128 devices in a mesh: space: 4 (over y_hi, core), filt: 32 (over y_lo, z, x).
Axes of the slice: x: 4, y: 4 (y_hi: 2, y_lo: 2; y = y_hi * 2 + y_lo), z: 4, core: 2. Of those that a mesh axis runs over, the one named last changes fastest.
Arguments:
- features: bfloat16 [256, 12, 2048], P('filt', 'space'), may hold values from -6 to 6
- weight: bfloat16 [256, 27, 256], P('filt'), may hold values from -0.078125 to 0.078125
- bias_vec: bfloat16 [256], P('filt'), may hold values from -3 to 3
- cotangent: bfloat16 [256, 12, 2048], P('filt', 'space'), may hold values from -6 to 6
Outputs:
- activation: bfloat16 [256, 12, 2048], P('filt', 'space')
- input_grad: bfloat16 [256, 12, 2048], P('filt', 'space')
- weight_grad: float32 [256, 27, 256], P('filt')
The draws below stay inside these ranges and needn't reach their ends.
All inputs are finite; a program needn't handle non-finite values.
Results may differ from the reference program's by a relative error of at most 0.014.
Values may be sent and summed in bfloat16 or wider, within the bound.
No kernel may reach another device: no remote copies, remote signals or barrier semaphores. Data moves between devices by JAX's collectives and lax.ppermute only.
A program may use at most 192 MiB of HBM per device.

```python
import math
import jax
import jax.numpy as jnp
from jax import lax

C = 256
H = 32
W = 64
DEPTH = 12


def levels(key, extent, shards, least, largest):
    def one(dim, shards_of):
        steps = jax.random.uniform(jax.random.fold_in(jax.random.fold_in(key, 6), dim), (shards_of,), jnp.float32, least / len(shards), largest / len(shards))
        return jnp.repeat(jnp.exp(steps), extent[dim] // shards_of).reshape((-1,) + (1,) * (len(extent) - dim - 1))

    gain = one(*shards[0])
    for cut in shards[1:]:
        gain = gain * one(*cut)
    return gain


def gaussian(key, dims, spread, limit, cuts=(), kind=jnp.bfloat16):
    gain = levels(key, dims, cuts, -0.22, 0.18) if cuts else 1.0
    array = jax.random.normal(key, dims, jnp.float32) * spread * gain
    return jnp.minimum(jnp.maximum(array, -limit), limit).astype(kind)


def setup_inputs(seed: int = 0) -> dict:
    streams_of = jax.random.split(jax.random.key(seed), 5)
    return {
        "features": gaussian(streams_of[0], (C, DEPTH, H * W), 1.0, 6.0, ((0, 32), (1, 4))),
        "weight": gaussian(streams_of[1], (C, 27, C), (27 * C) ** -0.5, 0.078125, ((0, 32),)),
        "bias_vec": gaussian(streams_of[2], (C,), 0.5, 3.0, ((0, 32),)),
        "cotangent": gaussian(streams_of[3], (C, DEPTH, H * W), 1.0, 6.0, ((0, 32), (1, 4))),
    }


DIMS = ('NCDHW', 'OIDHW', 'NCDHW')

def to_kernel(weight):
    grid = weight.reshape(weight.shape[0], 3, 3, 3, weight.shape[2])
    return jnp.transpose(grid, (0, 4, 1, 2, 3))

def flip_kernel(weight):
    flipped = weight[:, ::-1, :]
    grid = flipped.reshape(weight.shape[0], 3, 3, 3, weight.shape[2])
    return jnp.transpose(grid, (4, 0, 1, 2, 3))

def reference(features, weight, bias_vec, cotangent):
    volume = features.reshape(C, DEPTH, H, W)
    same = ((1, 1), (1, 1), (1, 1))
    pre_act = lax.conv_general_dilated(volume[None], to_kernel(weight), (1, 1, 1), same, dimension_numbers=DIMS, preferred_element_type=jnp.float32)[0]
    pre_act = pre_act + bias_vec.astype(jnp.float32)[:, None, None, None]
    sigmoid = jax.nn.sigmoid(pre_act)
    activation = (pre_act * sigmoid).astype(jnp.bfloat16)
    upstream = cotangent.reshape(C, DEPTH, H, W).astype(jnp.float32)
    pre_grad = (upstream * sigmoid * (1.0 + pre_act * (1.0 - sigmoid))).astype(jnp.bfloat16)
    input_grad = lax.conv_general_dilated(pre_grad[None], flip_kernel(weight), (1, 1, 1), same, dimension_numbers=DIMS, preferred_element_type=jnp.float32)[0]
    input_grad = input_grad.astype(jnp.bfloat16)
    padded = jnp.pad(volume, ((0, 0), (1, 1), (1, 1), (1, 1)))
    flat_grad = pre_grad.reshape(C, DEPTH * H * W)

    def offset_term(position):
        depth_at = position // 9
        row_at = position // 3 % 3
        col_at = position % 3
        anchor = jnp.zeros((), jnp.int32)
        window = lax.dynamic_slice(padded, (anchor, depth_at, row_at, col_at), (C, DEPTH, H, W))
        return jnp.dot(flat_grad, window.reshape(C, DEPTH * H * W).T, preferred_element_type=jnp.float32)
    terms = lax.map(offset_term, jnp.arange(27, dtype=jnp.int32))
    weight_grad = jnp.transpose(terms, (1, 0, 2)) * (1.0 / math.sqrt(DEPTH * H * W))
    return (activation.reshape(C, DEPTH, H * W), input_grad.reshape(C, DEPTH, H * W), weight_grad)
```

```python
import functools
import math

import jax
import jax.numpy as jnp
from jax import lax
from jax.experimental import pallas as pl
from jax.experimental.pallas import tpu as pltpu
from jax.sharding import PartitionSpec as P

H = 32
W = 64
PLANE = H * W
TAPS = [(kd, kh, kw) for kd in (-1, 0, 1) for kh in (-1, 0, 1) for kw in (-1, 0, 1)]


def moved(x, shift):
    return pltpu.roll(x, shift % x.shape[-1], x.ndim - 1) if shift else x


def columns(rows):
    lane = lax.broadcasted_iota(jnp.int32, (rows, PLANE), 1)
    return lane % W, lane // W


def forward_kernel(planes, block, x_ref, w_ref, own_ref, low_ref, high_ref, maps):
    w = w_ref[...]
    for d in range(planes):
        maps[d] = jnp.dot(
            w, x_ref[:, d * PLANE : (d + 1) * PLANE], preferred_element_type=jnp.float32
        )
    col, row = columns(block)
    for out in range(-1, planes + 1):
        total = None
        for kh in (-1, 0, 1):
            line = None
            for kw in (-1, 0, 1):
                term = None
                for kd in (-1, 0, 1):
                    if 0 <= out + kd < planes:
                        at = TAPS.index((kd, kh, kw)) * block
                        part = maps[out + kd, at : at + block, :]
                        term = part if term is None else term + part
                if kw:
                    inside = (col + kw >= 0) & (col + kw < W)
                    term = jnp.where(inside, moved(term, -kw), 0.0)
                line = term if line is None else line + term
            if kh:
                inside = (row + kh >= 0) & (row + kh < H)
                line = jnp.where(inside, moved(line, -kh * W), 0.0)
            total = line if total is None else total + line
        if out < 0:
            low_ref[...] = total
        elif out >= planes:
            high_ref[...] = total
        else:
            own_ref[:, out * PLANE : (out + 1) * PLANE] = total


def activate_kernel(planes, own_ref, before_ref, after_ref, bias_ref, cot_ref, act_ref, grad_ref):
    for d in range(planes):
        at = slice(d * PLANE, (d + 1) * PLANE)
        pre = own_ref[:, at]
        if d == 0:
            pre = pre + before_ref[...]
        if d == planes - 1:
            pre = pre + after_ref[...]
        pre = pre + bias_ref[...]
        s = jax.nn.sigmoid(pre)
        act_ref[:, at] = (pre * s).astype(act_ref.dtype)
        slope = s * (1.0 + pre * (1.0 - s))
        grad_ref[:, at] = (cot_ref[:, at].astype(jnp.float32) * slope).astype(grad_ref.dtype)


def backward_kernel(
    planes, block, grad_ref, before_ref, after_ref, x_ref, w_ref, part_ref, filt_ref, shifted, bank
):
    col, row = columns(block)
    for src in range(-1, planes + 1):
        if src < 0:
            g = before_ref[...]
        elif src >= planes:
            g = after_ref[...]
        else:
            g = grad_ref[:, src * PLANE : (src + 1) * PLANE]
        g = g.astype(jnp.float32)
        for kh in (-1, 0, 1):
            line = g
            if kh:
                inside = (row - kh >= 0) & (row - kh < H)
                line = jnp.where(inside, moved(g, kh * W), 0.0)
            for kw in (-1, 0, 1):
                term = line
                if kw:
                    inside = (col - kw >= 0) & (col - kw < W)
                    term = jnp.where(inside, moved(line, kw), 0.0)
                for kd in (-1, 0, 1):
                    if 0 <= src + kd < planes:
                        at = TAPS.index((kd, kh, kw)) * block
                        bank[src + kd, at : at + block, :] = term
    w = w_ref[...]
    total = None
    for d in range(planes):
        at = slice(d * PLANE, (d + 1) * PLANE)
        shifted[...] = bank[d].astype(jnp.bfloat16)
        part = lax.dot_general(
            shifted[...], x_ref[:, at], (((1,), (1,)), ((), ())), preferred_element_type=jnp.float32
        )
        total = part if total is None else total + part
        part_ref[:, at] = lax.dot_general(
            w, shifted[...], (((0,), (0,)), ((), ())), preferred_element_type=jnp.float32
        ).astype(part_ref.dtype)
    filt_ref[...] = total.astype(filt_ref.dtype)


def call(kernel, outs, scratch, flops, moved_bytes, name):
    return pl.pallas_call(
        kernel,
        out_shape=outs,
        scratch_shapes=scratch,
        compiler_params=pltpu.CompilerParams(vmem_limit_bytes=48 * 2**20),
        cost_estimate=pl.CostEstimate(flops=flops, bytes_accessed=moved_bytes, transcendentals=0),
        name=name,
    )


def neighbours(last, first):
    size = lax.axis_size("space")
    up = [(i, i + 1) for i in range(size - 1)]
    down = [(i + 1, i) for i in range(size - 1)]
    return lax.ppermute(last, "space", up), lax.ppermute(first, "space", down)


def per_device(features, weight, bias_vec, cotangent):
    block, planes, _ = features.shape
    channels = weight.shape[2]
    parts = lax.axis_size("filt")
    slabs = lax.axis_size("space")
    voxels = planes * PLANE
    rows = len(TAPS) * block
    x_own = features.reshape(block, voxels)
    w = jnp.transpose(weight, (1, 0, 2)).reshape(rows, channels)
    copies = jnp.broadcast_to(x_own[None], (parts, block, voxels))
    x = lax.all_to_all(copies, "filt", 0, 0, tiled=True).reshape(channels, voxels)

    plane_f32 = jax.ShapeDtypeStruct((block, PLANE), jnp.float32)
    flops = 2 * rows * channels * voxels
    own, low, high = call(
        functools.partial(forward_kernel, planes, block),
        (jax.ShapeDtypeStruct((block, voxels), jnp.float32), plane_f32, plane_f32),
        [pltpu.VMEM((planes, rows, PLANE), jnp.float32)],
        flops,
        2 * channels * voxels,
        "conv_forward",
    )(x, w)
    before, after = neighbours(high, low)
    half = jax.ShapeDtypeStruct((block, voxels), jnp.bfloat16)
    bias = jnp.broadcast_to(bias_vec.astype(jnp.float32)[:, None], (block, PLANE))
    activation, grad = call(
        functools.partial(activate_kernel, planes), (half, half), [], 20 * block * voxels, 12 * block * voxels, "activate"
    )(own, before, after, bias, cotangent.reshape(block, voxels))

    before, after = neighbours(grad[:, voxels - PLANE :], grad[:, :PLANE])
    part, filt = call(
        functools.partial(backward_kernel, planes, block),
        (
            jax.ShapeDtypeStruct((channels, voxels), jnp.bfloat16),
            jax.ShapeDtypeStruct((rows, channels), jnp.bfloat16),
        ),
        [
            pltpu.VMEM((rows, PLANE), jnp.bfloat16),
            pltpu.VMEM((planes, rows, PLANE), jnp.float32),
        ],
        2 * flops,
        4 * channels * voxels,
        "conv_backward",
    )(grad, before, after, x, w)
    scale = 1.0 / math.sqrt(planes * slabs * PLANE)
    weight_grad = lax.psum(filt, "space").astype(jnp.float32) * scale
    weight_grad = jnp.transpose(weight_grad.reshape(len(TAPS), block, channels), (1, 0, 2))
    got = lax.all_to_all(part.reshape(parts, block, voxels), "filt", 0, 0, tiled=True)
    input_grad = jnp.sum(got.astype(jnp.float32), axis=0).astype(jnp.bfloat16)
    shape = features.shape
    return activation.reshape(shape), input_grad.reshape(shape), weight_grad


def solution(mesh):
    return jax.shard_map(
        per_device,
        mesh=mesh,
        in_specs=(
            P("filt", "space", None),
            P("filt", None, None),
            P("filt"),
            P("filt", "space", None),
        ),
        out_specs=(P("filt", "space", None), P("filt", "space", None), P("filt", None, None)),
        check_vma=False,
    )
```

```python
import functools
import math

import jax
import jax.numpy as jnp
from jax import lax
from jax.experimental import pallas as pl
from jax.experimental.pallas import tpu as pltpu
from jax.sharding import PartitionSpec as P

H = 32
W = 64
PLANE = H * W
TAPS = [(kd, kh, kw) for kd in (-1, 0, 1) for kh in (-1, 0, 1) for kw in (-1, 0, 1)]
RING = 4
ROWS = H // RING
INNER = ROWS * W
OUTER = INNER + 2 * W
BLOCK = 8
WIDE = 256
TAP_ROWS = 224
F32 = jnp.float32
BF16 = jnp.bfloat16


def moved(x, shift):
    return pltpu.roll(x, shift % x.shape[-1], x.ndim - 1) if shift else x


def fold(x):
    return jnp.concatenate([x[:, :WIDE], x[:, WIDE:]], axis=0)


def unfold(x):
    return jnp.concatenate([x[:BLOCK], x[BLOCK:]], axis=1)


def inside_row(rows, kw):
    col = lax.broadcasted_iota(jnp.int32, (rows, OUTER), 1) % W
    return (col + kw >= 0) & (col + kw < W)


def pack_kernel(planes, at_ref, x_ref, cot_ref, w_ref, bias_ref, chunks_ref, *packs):
    w = jnp.concatenate([w_ref[...].astype(F32), jnp.zeros((BLOCK, WIDE), F32)], 0).astype(BF16)
    bias = bias_ref[...].astype(F32)
    bias = jnp.concatenate([bias, bias], 0).astype(BF16)
    for m, pack in enumerate(packs):
        pack[0:TAP_ROWS, :] = w
        chunk = jnp.bitwise_xor(at_ref[0], m)
        for d in range(planes):
            lanes = pl.ds(pl.multiple_of(chunk * INNER + d * PLANE, INNER), INNER)
            start = TAP_ROWS + 16 * d
            pack[start : start + 16, :] = fold(cot_ref[:, lanes].astype(F32)).astype(BF16)
        start = TAP_ROWS + 16 * planes
        pack[start : start + 16, :] = bias
    lane = lax.broadcasted_iota(jnp.int32, (BLOCK, 2 * W), 1)
    for v in range(RING):
        for d in range(planes):
            base = d * PLANE + v * INNER
            halo = jnp.zeros((BLOCK, 2 * W), F32)
            if v < RING - 1:
                below = x_ref[:, base + INNER : base + INNER + 2 * W].astype(F32)
                halo = jnp.where(lane < W, below, halo)
            if v > 0:
                above = x_ref[:, base - 2 * W : base].astype(F32)
                halo = jnp.where(lane < W, halo, above)
            own = x_ref[:, base : base + INNER]
            for g in range(chunks_ref.shape[0] // RING):
                chunks_ref[g * RING + v, :, d * OUTER : d * OUTER + INNER] = own
                chunks_ref[g * RING + v, :, d * OUTER + INNER : (d + 1) * OUTER] = halo.astype(BF16)


def forward_kernel(planes, x_ref, *refs):
    packs, (own_ref, low_ref, high_ref, up_ref, down_ref, maps) = refs[:RING], refs[RING:]
    for m in range(RING):
        maps[m] = jnp.dot(packs[m][0:TAP_ROWS, :], x_ref[...], preferred_element_type=F32)
    masks = {kw: inside_row(BLOCK, kw) for kw in (-1, 1)}
    for out in range(-1, planes + 1):
        pieces = []
        for m in range(RING):
            total = None
            for kh in (-1, 0, 1):
                line = None
                for kw in (-1, 0, 1):
                    term = None
                    for kd in (-1, 0, 1):
                        if 0 <= out + kd < planes:
                            at = TAPS.index((kd, kh, kw)) * BLOCK
                            d = out + kd
                            part = maps[m, at : at + BLOCK, d * OUTER : (d + 1) * OUTER]
                            term = part if term is None else term + part
                    if kw:
                        term = jnp.where(masks[kw], moved(term, -kw), 0.0)
                    line = term if line is None else line + term
                line = moved(line, -kh * W)
                total = line if total is None else total + line
            pieces.append(total[:, :INNER])
        total = jnp.concatenate(pieces, 0)
        if out < 0:
            low_ref[...] = total
            down_ref[:, 0:INNER] = total.astype(BF16)
        elif out >= planes:
            high_ref[...] = total
            up_ref[:, 0:INNER] = total.astype(BF16)
        else:
            own_ref[:, out * INNER : (out + 1) * INNER] = total
        for edge, ref in ((planes - 1, up_ref), (0, down_ref)):
            if out == edge:
                ref[:, INNER : 2 * INNER] = total.astype(BF16)
                ref[:, 2 * INNER : 3 * INNER] = upstream(packs, out).astype(BF16)


def upstream(packs, d):
    start = TAP_ROWS + 16 * d
    return jnp.concatenate([unfold(p[start : start + 16, :].astype(F32)) for p in packs], 0)


def backward_kernel(planes, x_ref, own_ref, low_ref, high_ref, before_ref, after_ref, *refs):
    packs, part_ref, backs = refs[:RING], refs[RING], refs[RING + 1 : 2 * RING + 1]
    bank, shifted = refs[2 * RING + 1 :]
    start = TAP_ROWS + 16 * planes
    bias = jnp.concatenate([p[start : start + BLOCK, 0:1].astype(F32) for p in packs], 0)
    masks = {kw: inside_row(BLOCK, kw) for kw in (-1, 1)}
    for m in range(RING):
        end = (m + 1) * TAP_ROWS
        bank[end - BLOCK : end, :] = jnp.zeros((BLOCK, planes * OUTER), F32)
    for src in range(-1, planes + 1):
        if src < 0:
            pre = before_ref[:, INNER : 2 * INNER].astype(F32) + low_ref[...]
            cot = before_ref[:, 2 * INNER : 3 * INNER].astype(F32)
        elif src >= planes:
            pre = after_ref[:, INNER : 2 * INNER].astype(F32) + high_ref[...]
            cot = after_ref[:, 2 * INNER : 3 * INNER].astype(F32)
        else:
            pre = own_ref[:, src * INNER : (src + 1) * INNER]
            cot = upstream(packs, src)
            if src == 0:
                pre = pre + before_ref[:, 0:INNER].astype(F32)
            if src == planes - 1:
                pre = pre + after_ref[:, 0:INNER].astype(F32)
        pre = pre + bias
        s = jax.nn.sigmoid(pre)
        if 0 <= src < planes:
            act = pre * s
            at = TAP_ROWS + 16 * src
            for m in range(RING):
                rows = act[m * BLOCK : (m + 1) * BLOCK]
                backs[m][at : at + 16, :] = fold(rows).astype(BF16)
        grad = (cot * (s * (1.0 + pre * (1.0 - s)))).astype(BF16).astype(F32)
        grad = jnp.concatenate([grad, jnp.zeros((grad.shape[0], 2 * W), F32)], 1)
        for m in range(RING):
            own = grad[m * BLOCK : (m + 1) * BLOCK]
            for kh in (-1, 0, 1):
                line = moved(own, kh * W)
                for kw in (-1, 0, 1):
                    term = line
                    if kw:
                        term = jnp.where(masks[-kw], moved(line, kw), 0.0)
                    for kd in (-1, 0, 1):
                        d = src + kd
                        if 0 <= d < planes:
                            at = m * TAP_ROWS + TAPS.index((kd, kh, kw)) * BLOCK
                            bank[at : at + BLOCK, d * OUTER : (d + 1) * OUTER] = term
    shifted[...] = bank[...].astype(BF16)
    filt = lax.dot_general(
        shifted[...], x_ref[...], (((1,), (1,)), ((), ())), preferred_element_type=F32
    )
    for m in range(RING):
        backs[m][0:TAP_ROWS, :] = filt[m * TAP_ROWS : (m + 1) * TAP_ROWS].astype(BF16)
    w = jnp.concatenate([p[0:TAP_ROWS, :] for p in packs], 0)
    part_ref[...] = lax.dot_general(
        w, shifted[...], (((0,), (0,)), ((), ())), preferred_element_type=F32
    ).astype(BF16)


def unpack_kernel(planes, at_ref, *refs):
    backs, (filt_ref, act_ref) = refs[:RING], refs[RING:]
    total = None
    for m, back in enumerate(backs):
        part = back[0:TAP_ROWS, :].astype(F32)
        total = part if total is None else total + part
        chunk = jnp.bitwise_xor(at_ref[0], m)
        for d in range(planes):
            lanes = pl.ds(pl.multiple_of(chunk * INNER + d * PLANE, INNER), INNER)
            start = TAP_ROWS + 16 * d
            act_ref[:, lanes] = unfold(back[start : start + 16, :].astype(F32)).astype(BF16)
    filt_ref[...] = total.astype(BF16)


def collect_kernel(planes, got_ref, out_ref):
    lane = lax.broadcasted_iota(jnp.int32, (BLOCK, 2 * W), 1)
    for d in range(planes):
        sums = []
        for v in range(RING):
            total = None
            for g in range(got_ref.shape[0] // RING):
                part = got_ref[g * RING + v, :, d * OUTER : (d + 1) * OUTER].astype(F32)
                total = part if total is None else total + part
            sums.append(total)
        for v in range(RING):
            first, last = sums[v][:, : 2 * W], sums[v][:, INNER - 2 * W : INNER]
            if v > 0:
                first = first + jnp.where(lane < W, sums[v - 1][:, INNER:], 0.0)
            if v < RING - 1:
                last = last + jnp.where(lane < W, 0.0, sums[v + 1][:, INNER:])
            whole = jnp.concatenate([first, sums[v][:, 2 * W : INNER - 2 * W], last], 1)
            base = d * PLANE + v * INNER
            out_ref[:, base : base + INNER] = whole.astype(BF16)


def call(kernel, ins, outs, scratch, flops, moved_bytes, name):
    smem = pl.BlockSpec(memory_space=pltpu.SMEM)
    vmem = pl.BlockSpec(memory_space=pltpu.VMEM)
    shapes = tuple(jax.ShapeDtypeStruct(shape, kind) for shape, kind in outs)
    return pl.pallas_call(
        kernel,
        out_shape=shapes,
        in_specs=[smem if x.dtype == jnp.int32 else vmem for x in ins],
        out_specs=tuple(vmem for _ in outs),
        scratch_shapes=scratch,
        compiler_params=pltpu.CompilerParams(vmem_limit_bytes=48 * 2**20),
        cost_estimate=pl.CostEstimate(flops=flops, bytes_accessed=moved_bytes, transcendentals=0),
        name=name,
    )(*ins)


def per_device(features, weight, bias_vec, cotangent):
    block, planes, _ = features.shape
    channels = weight.shape[2]
    parts = lax.axis_size("filt")
    slabs = lax.axis_size("space")
    voxels = planes * PLANE
    outer = planes * OUTER
    inner = planes * INNER
    group = RING * BLOCK
    at = (lax.axis_index("filt") % RING).astype(jnp.int32).reshape(1)
    w = jnp.transpose(weight, (1, 0, 2)).reshape(len(TAPS) * block, channels)
    bias = jnp.broadcast_to(bias_vec[:, None], (block, WIDE))
    pack = ((TAP_ROWS + 16 * planes + 16, WIDE), BF16)
    chunks, *packs = call(
        functools.partial(pack_kernel, planes),
        (at, features.reshape(block, voxels), cotangent.reshape(block, voxels), w, bias),
        [((parts, block, outer), BF16)] + [pack] * RING,
        [],
        0,
        2 * parts * block * outer,
        "pack",
    )

    def to_ring(values):
        swap = lambda m: [(i, i ^ m) for i in range(parts)]
        return [values[0]] + [lax.ppermute(values[m], "filt", swap(m)) for m in range(1, RING)]

    packs = to_ring(packs)
    x = lax.all_to_all(chunks, "filt", 0, 0, tiled=True).reshape(channels, outer)

    edge = ((group, 3 * INNER), BF16)
    plane = ((group, INNER), F32)
    flops = 2 * RING * TAP_ROWS * channels * outer
    own, low, high, up, down = call(
        functools.partial(forward_kernel, planes),
        (x, *packs),
        [((group, inner), F32), plane, plane, edge, edge],
        [pltpu.VMEM((RING, TAP_ROWS, outer), F32)],
        flops,
        2 * channels * outer,
        "conv_forward",
    )
    before = lax.ppermute(up, "space", [(i, i + 1) for i in range(slabs - 1)])
    after = lax.ppermute(down, "space", [(i + 1, i) for i in range(slabs - 1)])
    back = ((TAP_ROWS + 16 * planes, WIDE), BF16)
    part, *backs = call(
        functools.partial(backward_kernel, planes),
        (x, own, low, high, before, after, *packs),
        [((channels, outer), BF16)] + [back] * RING,
        [
            pltpu.VMEM((RING * TAP_ROWS, outer), F32),
            pltpu.VMEM((RING * TAP_ROWS, outer), BF16),
        ],
        2 * flops,
        4 * channels * outer,
        "conv_backward",
    )
    backs = to_ring(backs)
    got = lax.all_to_all(part.reshape(parts, block, outer), "filt", 0, 0, tiled=True)
    filt, activation = call(
        functools.partial(unpack_kernel, planes),
        (at, *backs),
        [((TAP_ROWS, WIDE), BF16), ((block, voxels), BF16)],
        [],
        0,
        RING * TAP_ROWS * WIDE * 2,
        "unpack",
    )
    for m in (1, 2):
        other = lax.ppermute(filt, "space", [(i, i ^ m) for i in range(slabs)])
        filt = filt.astype(F32) + other.astype(F32)
        filt = filt.astype(BF16) if m == 1 else filt * (1.0 / math.sqrt(planes * slabs * PLANE))
    weight_grad = filt[: len(TAPS) * block].reshape(len(TAPS), block, channels)
    (input_grad,) = call(
        functools.partial(collect_kernel, planes),
        (got,),
        [((block, voxels), BF16)],
        [],
        0,
        2 * channels * outer,
        "collect",
    )
    shape = features.shape
    return (
        activation.reshape(shape),
        input_grad.reshape(shape),
        jnp.transpose(weight_grad, (1, 0, 2)),
    )


def solution(mesh):
    return jax.shard_map(
        per_device,
        mesh=mesh,
        in_specs=(
            P("filt", "space", None),
            P("filt", None, None),
            P("filt"),
            P("filt", "space", None),
        ),
        out_specs=(P("filt", "space", None), P("filt", "space", None), P("filt", None, None)),
        check_vma=False,
    )
```

```python
import functools
import math

import jax
import jax.numpy as jnp
from jax import lax
from jax.experimental import pallas as pl
from jax.experimental.pallas import tpu as pltpu
from jax.sharding import PartitionSpec as P

H = 32
W = 64
PLANE = H * W
TAPS = [(kd, kh, kw) for kd in (-1, 0, 1) for kh in (-1, 0, 1) for kw in (-1, 0, 1)]
RING = 4
ROWS = H // RING
INNER = ROWS * W
OUTER = INNER + 2 * W
BLOCK = 8
WIDE = 256
TAP_ROWS = 224
PREPARE = 16 * 10**9
UNPACK = 16 * 10**9
F32 = jnp.float32
BF16 = jnp.bfloat16


def moved(x, shift):
    return pltpu.roll(x, shift % x.shape[-1], x.ndim - 1) if shift else x


def fold(x):
    return jnp.concatenate([x[:, :WIDE], x[:, WIDE:]], axis=0)


def unfold(x):
    return jnp.concatenate([x[:BLOCK], x[BLOCK:]], axis=1)


def inside_row(rows, kw):
    col = lax.broadcasted_iota(jnp.int32, (rows, OUTER), 1) % W
    return (col + kw >= 0) & (col + kw < W)


def pack_kernel(planes, at_ref, x_any, cot_any, w_any, bias_ref, chunks_ref, *refs):
    packs, (x_ref, cot_ref, w_ref, sems) = refs[:RING], refs[RING:]
    copies = [
        pltpu.make_async_copy(src, dst, sems.at[i])
        for i, (src, dst) in enumerate(((w_any, w_ref), (cot_any, cot_ref), (x_any, x_ref)))
    ]
    for copy in copies:
        copy.start()
    bias = jnp.broadcast_to(bias_ref[...].astype(F32), (16, BLOCK))
    bias = jnp.concatenate([bias, jnp.zeros((16, WIDE - BLOCK), F32)], 1).astype(BF16)
    copies[0].wait()
    w = jnp.concatenate([w_ref[...].astype(F32), jnp.zeros((BLOCK, WIDE), F32)], 0).astype(BF16)
    for pack in packs:
        pack[0:TAP_ROWS, :] = w
    copies[1].wait()
    for m, pack in enumerate(packs):
        chunk = jnp.bitwise_xor(at_ref[0], m)
        for d in range(planes):
            lanes = pl.ds(pl.multiple_of(chunk * INNER + d * PLANE, INNER), INNER)
            start = TAP_ROWS + 16 * d
            pack[start : start + 16, :] = fold(cot_ref[:, lanes].astype(F32)).astype(BF16)
        start = TAP_ROWS + 16 * planes
        pack[start : start + 16, :] = bias
    copies[2].wait()
    lane = lax.broadcasted_iota(jnp.int32, (BLOCK, 2 * W), 1)
    for v in range(RING):
        for d in range(planes):
            base = d * PLANE + v * INNER
            halo = jnp.zeros((BLOCK, 2 * W), F32)
            if v < RING - 1:
                below = x_ref[:, base + INNER : base + INNER + 2 * W].astype(F32)
                halo = jnp.where(lane < W, below, halo)
            if v > 0:
                above = x_ref[:, base - 2 * W : base].astype(F32)
                halo = jnp.where(lane < W, halo, above)
            own = x_ref[:, base : base + INNER]
            for g in range(chunks_ref.shape[0] // RING):
                chunks_ref[g * RING + v, :, d * OUTER : d * OUTER + INNER] = own
                chunks_ref[g * RING + v, :, d * OUTER + INNER : (d + 1) * OUTER] = halo.astype(BF16)


def prepare_kernel(planes, *refs):
    packs, (w_ref, turned_ref, cot_ref, bias_ref) = refs[:RING], refs[RING:]
    diagonal = lax.broadcasted_iota(jnp.int32, (BLOCK, 2 * W), 0) == lax.broadcasted_iota(
        jnp.int32, (BLOCK, 2 * W), 1
    )
    for m, pack in enumerate(packs):
        own = slice(m * BLOCK, (m + 1) * BLOCK)
        w_ref[m * TAP_ROWS : (m + 1) * TAP_ROWS, :] = pack[0:TAP_ROWS, :]
        for d in range(planes):
            start = TAP_ROWS + 16 * d
            lanes = slice(d * INNER, (d + 1) * INNER)
            cot_ref[own, lanes] = unfold(pack[start : start + 16, :].astype(F32))
        start = TAP_ROWS + 16 * planes
        row = pack[start : start + 16, 0 : 2 * W].astype(F32)[:BLOCK]
        bias = jnp.sum(jnp.where(diagonal, row, 0.0), axis=1, keepdims=True)
        bias_ref[own, :] = jnp.broadcast_to(bias, (BLOCK, 2 * W))
    turned_ref[...] = w_ref[...].T


def forward_kernel(
    planes, x_ref, w_ref, cot_ref, own_ref, low_ref, high_ref, up_ref, down_ref, maps
):
    maps[...] = jnp.dot(w_ref[...], x_ref[...], preferred_element_type=F32)
    masks = {kw: inside_row(BLOCK, kw) for kw in (-1, 1)}
    for out in range(-1, planes + 1):
        pieces = []
        for m in range(RING):
            total = None
            for kh in (-1, 0, 1):
                line = None
                for kw in (-1, 0, 1):
                    term = None
                    for kd in (-1, 0, 1):
                        if 0 <= out + kd < planes:
                            at = m * TAP_ROWS + TAPS.index((kd, kh, kw)) * BLOCK
                            d = out + kd
                            part = maps[at : at + BLOCK, d * OUTER : (d + 1) * OUTER]
                            term = part if term is None else term + part
                    if kw:
                        term = jnp.where(masks[kw], moved(term, -kw), 0.0)
                    line = term if line is None else line + term
                line = moved(line, -kh * W)
                total = line if total is None else total + line
            pieces.append(total[:, :INNER])
        total = jnp.concatenate(pieces, 0)
        if out < 0:
            low_ref[...] = total
            down_ref[:, 0:INNER] = total.astype(BF16)
        elif out >= planes:
            high_ref[...] = total
            up_ref[:, 0:INNER] = total.astype(BF16)
        else:
            own_ref[:, out * INNER : (out + 1) * INNER] = total
        for edge, ref in ((planes - 1, up_ref), (0, down_ref)):
            if out == edge:
                ref[:, INNER : 2 * INNER] = total.astype(BF16)
                ref[:, 2 * INNER : 3 * INNER] = cot_ref[
                    :, out * INNER : (out + 1) * INNER
                ].astype(BF16)


def backward_kernel(
    planes, x_ref, own_ref, low_ref, high_ref, before_ref, after_ref, cot_ref, bias_ref, *refs
):
    shifted, backs, bank = refs[0], refs[1 : RING + 1], refs[RING + 1]
    bias = bias_ref[:, 0:1]
    masks = {kw: inside_row(BLOCK, kw) for kw in (-1, 1)}
    for m in range(RING):
        end = (m + 1) * TAP_ROWS
        bank[end - BLOCK : end, :] = jnp.zeros((BLOCK, planes * OUTER), F32)
    for src in range(-1, planes + 1):
        if src < 0:
            pre = before_ref[:, INNER : 2 * INNER].astype(F32) + low_ref[...]
            cot = before_ref[:, 2 * INNER : 3 * INNER].astype(F32)
        elif src >= planes:
            pre = after_ref[:, INNER : 2 * INNER].astype(F32) + high_ref[...]
            cot = after_ref[:, 2 * INNER : 3 * INNER].astype(F32)
        else:
            pre = own_ref[:, src * INNER : (src + 1) * INNER]
            cot = cot_ref[:, src * INNER : (src + 1) * INNER]
            if src == 0:
                pre = pre + before_ref[:, 0:INNER].astype(F32)
            if src == planes - 1:
                pre = pre + after_ref[:, 0:INNER].astype(F32)
        pre = pre + bias
        s = jax.nn.sigmoid(pre)
        if 0 <= src < planes:
            act = pre * s
            at = TAP_ROWS + 16 * src
            for m in range(RING):
                rows = act[m * BLOCK : (m + 1) * BLOCK]
                backs[m][at : at + 16, :] = fold(rows).astype(BF16)
        grad = (cot * (s * (1.0 + pre * (1.0 - s)))).astype(BF16).astype(F32)
        grad = jnp.concatenate([grad, jnp.zeros((grad.shape[0], 2 * W), F32)], 1)
        for m in range(RING):
            own = grad[m * BLOCK : (m + 1) * BLOCK]
            for kh in (-1, 0, 1):
                line = moved(own, kh * W)
                for kw in (-1, 0, 1):
                    term = line
                    if kw:
                        term = jnp.where(masks[-kw], moved(line, kw), 0.0)
                    for kd in (-1, 0, 1):
                        d = src + kd
                        if 0 <= d < planes:
                            at = m * TAP_ROWS + TAPS.index((kd, kh, kw)) * BLOCK
                            bank[at : at + BLOCK, d * OUTER : (d + 1) * OUTER] = term
    shifted[...] = bank[...].astype(BF16)
    filt = lax.dot_general(
        shifted[...], x_ref[...], (((1,), (1,)), ((), ())), preferred_element_type=F32
    )
    for m in range(RING):
        backs[m][0:TAP_ROWS, :] = filt[m * TAP_ROWS : (m + 1) * TAP_ROWS].astype(BF16)


def input_kernel(turned_ref, shifted, part_ref):
    part = jnp.dot(turned_ref[...], shifted[...], preferred_element_type=F32)
    part_ref[...] = part.astype(BF16)


def unpack_kernel(planes, at_ref, *refs):
    backs, (filt_ref, act_ref) = refs[:RING], refs[RING:]
    total = None
    for m, back in enumerate(backs):
        part = back[0:TAP_ROWS, :].astype(F32)
        total = part if total is None else total + part
        chunk = jnp.bitwise_xor(at_ref[0], m)
        for d in range(planes):
            lanes = pl.ds(pl.multiple_of(chunk * INNER + d * PLANE, INNER), INNER)
            start = TAP_ROWS + 16 * d
            act_ref[:, lanes] = unfold(back[start : start + 16, :].astype(F32)).astype(BF16)
    filt_ref[...] = total.astype(BF16)


def collect_kernel(planes, got_ref, out_ref):
    lane = lax.broadcasted_iota(jnp.int32, (BLOCK, 2 * W), 1)
    for d in range(planes):
        sums = []
        for v in range(RING):
            total = None
            for g in range(got_ref.shape[0] // RING):
                part = got_ref[g * RING + v, :, d * OUTER : (d + 1) * OUTER].astype(F32)
                total = part if total is None else total + part
            sums.append(total)
        for v in range(RING):
            first, last = sums[v][:, : 2 * W], sums[v][:, INNER - 2 * W : INNER]
            if v > 0:
                first = first + jnp.where(lane < W, sums[v - 1][:, INNER:], 0.0)
            if v < RING - 1:
                last = last + jnp.where(lane < W, 0.0, sums[v + 1][:, INNER:])
            whole = jnp.concatenate([first, sums[v][:, 2 * W : INNER - 2 * W], last], 1)
            base = d * PLANE + v * INNER
            out_ref[:, base : base + INNER] = whole.astype(BF16)


def call(kernel, ins, outs, scratch, flops, moved_bytes, name, hbm=(), limit=48):
    smem = pl.BlockSpec(memory_space=pltpu.SMEM)
    vmem = pl.BlockSpec(memory_space=pltpu.VMEM)
    anywhere = pl.BlockSpec(memory_space=pl.ANY)
    shapes = tuple(jax.ShapeDtypeStruct(shape, kind) for shape, kind in outs)
    return pl.pallas_call(
        kernel,
        out_shape=shapes,
        in_specs=[smem if x.dtype == jnp.int32 else anywhere if i in hbm else vmem for i, x in enumerate(ins)],
        out_specs=tuple(vmem for _ in outs),
        scratch_shapes=scratch,
        compiler_params=pltpu.CompilerParams(vmem_limit_bytes=limit * 2**20),
        cost_estimate=pl.CostEstimate(flops=flops, bytes_accessed=moved_bytes, transcendentals=0),
        name=name,
    )(*ins)


def per_device(features, weight, bias_vec, cotangent):
    block, planes, _ = features.shape
    channels = weight.shape[2]
    parts = lax.axis_size("filt")
    slabs = lax.axis_size("space")
    voxels = planes * PLANE
    outer = planes * OUTER
    inner = planes * INNER
    group = RING * BLOCK
    at = jnp.bitwise_and(lax.axis_index("filt"), RING - 1).astype(jnp.int32).reshape(1)
    w = jnp.transpose(weight, (1, 0, 2)).reshape(len(TAPS) * block, channels)
    pack = ((TAP_ROWS + 16 * planes + 16, WIDE), BF16)
    chunks, *packs = call(
        functools.partial(pack_kernel, planes),
        (at, features.reshape(block, voxels), cotangent.reshape(block, voxels), w, bias_vec[None]),
        [((parts, block, outer), BF16)] + [pack] * RING,
        [
            pltpu.VMEM((block, voxels), BF16),
            pltpu.VMEM((block, voxels), BF16),
            pltpu.VMEM((len(TAPS) * block, channels), BF16),
            pltpu.SemaphoreType.DMA((3,)),
        ],
        0,
        2 * parts * block * outer,
        "pack",
        (1, 2, 3),
        61,
    )

    def to_ring(values):
        swap = lambda m: [(i, i ^ m) for i in range(parts)]
        return [values[0]] + [lax.ppermute(values[m], "filt", swap(m)) for m in range(1, RING)]

    packs = to_ring(packs)
    x = lax.all_to_all(chunks, "filt", 0, 0, tiled=True).reshape(channels, outer)

    edge = ((group, 3 * INNER), BF16)
    plane = ((group, INNER), F32)
    flops = 2 * RING * TAP_ROWS * channels * outer
    w, turned, cot, bias = call(
        functools.partial(prepare_kernel, planes),
        packs,
        [
            ((RING * TAP_ROWS, channels), BF16),
            ((channels, RING * TAP_ROWS), BF16),
            ((group, inner), F32),
            ((group, 2 * W), F32),
        ],
        [],
        PREPARE,
        RING * TAP_ROWS * WIDE * 4,
        "prepare",
    )
    own, low, high, up, down = call(
        functools.partial(forward_kernel, planes),
        (x, w, cot),
        [((group, inner), F32), plane, plane, edge, edge],
        [pltpu.VMEM((RING * TAP_ROWS, outer), F32)],
        flops,
        2 * channels * outer,
        "conv_forward",
    )
    before = lax.ppermute(up, "space", [(i, i + 1) for i in range(slabs - 1)])
    after = lax.ppermute(down, "space", [(i + 1, i) for i in range(slabs - 1)])
    back = ((TAP_ROWS + 16 * planes, WIDE), BF16)
    shifted, *backs = call(
        functools.partial(backward_kernel, planes),
        (x, own, low, high, before, after, cot, bias),
        [((RING * TAP_ROWS, outer), BF16)] + [back] * RING,
        [pltpu.VMEM((RING * TAP_ROWS, outer), F32)],
        flops,
        4 * channels * outer,
        "filter_gradient",
    )
    backs = to_ring(backs)
    (part,) = call(
        input_kernel,
        (turned, shifted),
        [((channels, outer), BF16)],
        [],
        flops,
        4 * channels * outer,
        "input_gradient",
    )
    got = lax.all_to_all(part.reshape(parts, block, outer), "filt", 0, 0, tiled=True)
    filt, activation = call(
        functools.partial(unpack_kernel, planes),
        (at, *backs),
        [((TAP_ROWS, WIDE), BF16), ((block, voxels), BF16)],
        [],
        UNPACK,
        RING * TAP_ROWS * WIDE * 2,
        "unpack",
    )
    for m in (1, 2):
        other = lax.ppermute(filt, "space", [(i, i ^ m) for i in range(slabs)])
        filt = filt.astype(F32) + other.astype(F32)
        filt = filt.astype(BF16) if m == 1 else filt * (1.0 / math.sqrt(planes * slabs * PLANE))
    weight_grad = filt[: len(TAPS) * block].reshape(len(TAPS), block, channels)
    (input_grad,) = call(
        functools.partial(collect_kernel, planes),
        (got,),
        [((block, voxels), BF16)],
        [],
        0,
        2 * channels * outer,
        "collect",
    )
    shape = features.shape
    return (
        activation.reshape(shape),
        input_grad.reshape(shape),
        jnp.transpose(weight_grad, (1, 0, 2)),
    )


def solution(mesh):
    return jax.shard_map(
        per_device,
        mesh=mesh,
        in_specs=(
            P("filt", "space", None),
            P("filt", None, None),
            P("filt"),
            P("filt", "space", None),
        ),
        out_specs=(P("filt", "space", None), P("filt", "space", None), P("filt", None, None)),
        check_vma=False,
    )
```

```python
import functools
import math

import jax
import jax.numpy as jnp
from jax import lax
from jax.experimental import pallas as pl
from jax.experimental.pallas import tpu as pltpu
from jax.sharding import PartitionSpec as P

H = 32
W = 64
PLANE = H * W
TAPS = [(kd, kh, kw) for kd in (-1, 0, 1) for kh in (-1, 0, 1) for kw in (-1, 0, 1)]
RING = 4
ROWS = H // RING
INNER = ROWS * W
OUTER = INNER + 2 * W
BLOCK = 8
WIDE = 256
TAP_ROWS = 224
PREPARE = 16 * 10**9
UNPACK = 16 * 10**9
F32 = jnp.float32
BF16 = jnp.bfloat16


def moved(x, shift):
    return pltpu.roll(x, shift % x.shape[-1], x.ndim - 1) if shift else x


def fold(x):
    return jnp.concatenate([x[:, :WIDE], x[:, WIDE:]], axis=0)


def unfold(x):
    return jnp.concatenate([x[:BLOCK], x[BLOCK:]], axis=1)


def inside_row(rows, kw):
    col = lax.broadcasted_iota(jnp.int32, (rows, OUTER), 1) % W
    return (col + kw >= 0) & (col + kw < W)


def pack_kernel(planes, x_any, cot_any, w_any, bias_any, chunks, *refs):
    packs, (x_ref, cot_ref, w_ref, bias_ref, in_sems) = refs[:RING], refs[RING:]
    copies = [
        pltpu.make_async_copy(src, dst, in_sems.at[i])
        for i, (src, dst) in enumerate(((w_any, w_ref), (x_any, x_ref), (cot_any, cot_ref), (bias_any, bias_ref)))
    ]
    for copy in copies:
        copy.start()
    copies[0].wait()
    w = jnp.concatenate([w_ref[...].astype(F32), jnp.zeros((BLOCK, WIDE), F32)], 0).astype(BF16)
    for m in range(RING):
        packs[m][0:TAP_ROWS, :] = w
    copies[1].wait()
    lane = lax.broadcasted_iota(jnp.int32, (BLOCK, 2 * W), 1)
    for v in range(RING):
        for d in range(planes):
            base = d * PLANE + v * INNER
            halo = jnp.zeros((BLOCK, 2 * W), F32)
            if v < RING - 1:
                below = x_ref[:, base + INNER : base + INNER + 2 * W].astype(F32)
                halo = jnp.where(lane < W, below, halo)
            if v > 0:
                above = x_ref[:, base - 2 * W : base].astype(F32)
                halo = jnp.where(lane < W, halo, above)
            own, halo = x_ref[:, base : base + INNER], halo.astype(BF16)
            for g in range(chunks.shape[0] // RING):
                chunks[g * RING + v, :, d * OUTER : d * OUTER + INNER] = own
                chunks[g * RING + v, :, d * OUTER + INNER : (d + 1) * OUTER] = halo
    copies[2].wait()
    copies[3].wait()
    bias = jnp.broadcast_to(bias_ref[...].astype(F32), (16, BLOCK))
    bias = jnp.concatenate([bias, jnp.zeros((16, WIDE - BLOCK), F32)], 1).astype(BF16)
    for m in range(RING):
        chunk = jnp.bitwise_xor(jnp.bitwise_and(lax.axis_index("filt"), RING - 1), m)
        for d in range(planes):
            lanes = pl.ds(pl.multiple_of(chunk * INNER + d * PLANE, INNER), INNER)
            start = TAP_ROWS + 16 * d
            packs[m][start : start + 16, :] = fold(cot_ref[:, lanes].astype(F32)).astype(BF16)
        start = TAP_ROWS + 16 * planes
        packs[m][start : start + 16, :] = bias


def prepare_kernel(planes, *refs):
    packs, (w_ref, turned_ref, cot_ref, bias_ref) = refs[:RING], refs[RING:]
    diagonal = lax.broadcasted_iota(jnp.int32, (BLOCK, 2 * W), 0) == lax.broadcasted_iota(
        jnp.int32, (BLOCK, 2 * W), 1
    )
    for m, pack in enumerate(packs):
        own = slice(m * BLOCK, (m + 1) * BLOCK)
        w_ref[m * TAP_ROWS : (m + 1) * TAP_ROWS, :] = pack[0:TAP_ROWS, :]
        for d in range(planes):
            start = TAP_ROWS + 16 * d
            lanes = slice(d * INNER, (d + 1) * INNER)
            cot_ref[own, lanes] = unfold(pack[start : start + 16, :].astype(F32))
        start = TAP_ROWS + 16 * planes
        row = pack[start : start + 16, 0 : 2 * W].astype(F32)[:BLOCK]
        bias = jnp.sum(jnp.where(diagonal, row, 0.0), axis=1, keepdims=True)
        bias_ref[own, :] = jnp.broadcast_to(bias, (BLOCK, 2 * W))
    turned_ref[...] = w_ref[...].T


def forward_kernel(
    planes, x_ref, w_ref, cot_ref, own_ref, low_ref, high_ref, up_ref, down_ref, *maps
):
    for m in range(RING):
        w = w_ref[m * TAP_ROWS : (m + 1) * TAP_ROWS, :]
        maps[m][...] = jnp.dot(w, x_ref[...], preferred_element_type=F32)
    masks = {kw: inside_row(BLOCK, kw) for kw in (-1, 1)}
    for out in range(-1, planes + 1):
        pieces = []
        for m in range(RING):
            total = None
            for kh in (-1, 0, 1):
                line = None
                for kw in (-1, 0, 1):
                    term = None
                    for kd in (-1, 0, 1):
                        if 0 <= out + kd < planes:
                            at = TAPS.index((kd, kh, kw)) * BLOCK
                            d = out + kd
                            part = maps[m][at : at + BLOCK, d * OUTER : (d + 1) * OUTER]
                            term = part if term is None else term + part
                    if kw:
                        term = jnp.where(masks[kw], moved(term, -kw), 0.0)
                    line = term if line is None else line + term
                line = moved(line, -kh * W)
                total = line if total is None else total + line
            pieces.append(total[:, :INNER])
        total = jnp.concatenate(pieces, 0)
        if out < 0:
            low_ref[...] = total
            down_ref[:, 0:INNER] = total.astype(BF16)
        elif out >= planes:
            high_ref[...] = total
            up_ref[:, 0:INNER] = total.astype(BF16)
        else:
            own_ref[:, out * INNER : (out + 1) * INNER] = total
        for edge, ref in ((planes - 1, up_ref), (0, down_ref)):
            if out == edge:
                ref[:, INNER : 2 * INNER] = total.astype(BF16)
                ref[:, 2 * INNER : 3 * INNER] = cot_ref[
                    :, out * INNER : (out + 1) * INNER
                ].astype(BF16)


def backward_kernel(
    planes, x_ref, own_ref, low_ref, high_ref, before_ref, after_ref, cot_ref, bias_ref, *refs
):
    turned_ref, part_any, backs = refs[0], refs[1], refs[2 : RING + 2]
    bank, (shifted, part, sems) = refs[RING + 2 : 2 * RING + 2], refs[2 * RING + 2 :]
    bias = bias_ref[:, 0:1]
    masks = {kw: inside_row(BLOCK, kw) for kw in (-1, 1)}
    for m in range(RING):
        bank[m][TAP_ROWS - BLOCK : TAP_ROWS, :] = jnp.zeros((BLOCK, planes * OUTER), F32)
    for src in range(-1, planes + 1):
        if src < 0:
            pre = before_ref[:, INNER : 2 * INNER].astype(F32) + low_ref[...]
            cot = before_ref[:, 2 * INNER : 3 * INNER].astype(F32)
        elif src >= planes:
            pre = after_ref[:, INNER : 2 * INNER].astype(F32) + high_ref[...]
            cot = after_ref[:, 2 * INNER : 3 * INNER].astype(F32)
        else:
            pre = own_ref[:, src * INNER : (src + 1) * INNER]
            cot = cot_ref[:, src * INNER : (src + 1) * INNER]
            if src == 0:
                pre = pre + before_ref[:, 0:INNER].astype(F32)
            if src == planes - 1:
                pre = pre + after_ref[:, 0:INNER].astype(F32)
        pre = pre + bias
        s = jax.nn.sigmoid(pre)
        if 0 <= src < planes:
            act = pre * s
            at = TAP_ROWS + 16 * src
            for m in range(RING):
                rows = act[m * BLOCK : (m + 1) * BLOCK]
                backs[m][at : at + 16, :] = fold(rows).astype(BF16)
        grad = (cot * (s * (1.0 + pre * (1.0 - s)))).astype(BF16).astype(F32)
        grad = jnp.concatenate([grad, jnp.zeros((grad.shape[0], 2 * W), F32)], 1)
        for m in range(RING):
            own = grad[m * BLOCK : (m + 1) * BLOCK]
            for kh in (-1, 0, 1):
                line = moved(own, kh * W)
                for kw in (-1, 0, 1):
                    term = line
                    if kw:
                        term = jnp.where(masks[-kw], moved(line, kw), 0.0)
                    for kd in (-1, 0, 1):
                        d = src + kd
                        if 0 <= d < planes:
                            at = TAPS.index((kd, kh, kw)) * BLOCK
                            bank[m][at : at + BLOCK, d * OUTER : (d + 1) * OUTER] = term
    for m in range(RING):
        rows = slice(m * TAP_ROWS, (m + 1) * TAP_ROWS)
        shifted[rows, :] = bank[m][...].astype(BF16)
        filt = lax.dot_general(
            shifted[rows, :], x_ref[...], (((1,), (1,)), ((), ())), preferred_element_type=F32
        )
        backs[m][0:TAP_ROWS, :] = filt.astype(BF16)
    copies = []
    for d in range(planes):
        lanes = slice(d * OUTER, (d + 1) * OUTER)
        total = jnp.dot(turned_ref[...], shifted[:, lanes], preferred_element_type=F32)
        part[:, lanes] = total.astype(BF16)
        copies.append(pltpu.make_async_copy(part.at[:, lanes], part_any.at[:, lanes], sems.at[d]))
        copies[-1].start()
    for copy in copies:
        copy.wait()


def unpack_kernel(planes, *refs):
    backs, (filt_ref, act_ref) = refs[:RING], refs[RING:]
    total = None
    for m, back in enumerate(backs):
        part = back[0:TAP_ROWS, :].astype(F32)
        total = part if total is None else total + part
        chunk = jnp.bitwise_xor(jnp.bitwise_and(lax.axis_index("filt"), RING - 1), m)
        for d in range(planes):
            lanes = pl.ds(pl.multiple_of(chunk * INNER + d * PLANE, INNER), INNER)
            start = TAP_ROWS + 16 * d
            act_ref[:, lanes] = unfold(back[start : start + 16, :].astype(F32)).astype(BF16)
    filt_ref[...] = total.astype(BF16)


def collect_kernel(planes, scale, got_ref, filt_ref, other_ref, out_ref, weight_ref):
    rows = weight_ref.shape[0]
    filt = filt_ref[...].astype(F32) + other_ref[...].astype(F32)
    weight_ref[...] = (filt * scale)[:rows]
    lane = lax.broadcasted_iota(jnp.int32, (BLOCK, 2 * W), 1)
    for d in range(planes):
        sums = []
        for v in range(RING):
            total = None
            for g in range(got_ref.shape[0] // RING):
                part = got_ref[g * RING + v, :, d * OUTER : (d + 1) * OUTER].astype(F32)
                total = part if total is None else total + part
            sums.append(total)
        for v in range(RING):
            first, last = sums[v][:, : 2 * W], sums[v][:, INNER - 2 * W : INNER]
            if v > 0:
                first = first + jnp.where(lane < W, sums[v - 1][:, INNER:], 0.0)
            if v < RING - 1:
                last = last + jnp.where(lane < W, 0.0, sums[v + 1][:, INNER:])
            whole = jnp.concatenate([first, sums[v][:, 2 * W : INNER - 2 * W], last], 1)
            base = d * PLANE + v * INNER
            out_ref[:, base : base + INNER] = whole.astype(BF16)


def call(kernel, ins, outs, scratch, flops, moved_bytes, name, hbm=(), outs_hbm=(), limit=48):
    smem = pl.BlockSpec(memory_space=pltpu.SMEM)
    vmem = pl.BlockSpec(memory_space=pltpu.VMEM)
    anywhere = pl.BlockSpec(memory_space=pl.ANY)
    shapes = tuple(jax.ShapeDtypeStruct(shape, kind) for shape, kind in outs)
    return pl.pallas_call(
        kernel,
        out_shape=shapes,
        in_specs=[smem if x.dtype == jnp.int32 else anywhere if i in hbm else vmem for i, x in enumerate(ins)],
        out_specs=tuple(anywhere if i in outs_hbm else vmem for i in range(len(outs))),
        scratch_shapes=scratch,
        compiler_params=pltpu.CompilerParams(vmem_limit_bytes=limit * 2**20),
        cost_estimate=pl.CostEstimate(flops=flops, bytes_accessed=moved_bytes, transcendentals=0),
        name=name,
    )(*ins)


def per_device(features, weight, bias_vec, cotangent):
    block, planes, _ = features.shape
    channels = weight.shape[2]
    parts = lax.axis_size("filt")
    slabs = lax.axis_size("space")
    voxels = planes * PLANE
    outer = planes * OUTER
    inner = planes * INNER
    group = RING * BLOCK
    w = jnp.transpose(weight, (1, 0, 2)).reshape(len(TAPS) * block, channels)
    pack = ((TAP_ROWS + 16 * planes + 16, WIDE), BF16)
    chunks, *packs = call(
        functools.partial(pack_kernel, planes),
        (features.reshape(block, voxels), cotangent.reshape(block, voxels), w, bias_vec[None]),
        [((parts, block, outer), BF16)] + [pack] * RING,
        [
            pltpu.VMEM((block, voxels), BF16),
            pltpu.VMEM((block, voxels), BF16),
            pltpu.VMEM((len(TAPS) * block, channels), BF16),
            pltpu.VMEM((1, block), BF16),
            pltpu.SemaphoreType.DMA((4,)),
        ],
        0,
        2 * parts * block * outer,
        "pack",
        (0, 1, 2, 3),
        (),
        61,
    )

    def to_ring(values):
        swap = lambda m: [(i, i ^ m) for i in range(parts)]
        return [values[0]] + [lax.ppermute(values[m], "filt", swap(m)) for m in range(1, RING)]

    packs = to_ring(packs)
    x = lax.all_to_all(chunks, "filt", 0, 0, tiled=True).reshape(channels, outer)

    edge = ((group, 3 * INNER), BF16)
    plane = ((group, INNER), F32)
    flops = 2 * RING * TAP_ROWS * channels * outer
    w, turned, cot, bias = call(
        functools.partial(prepare_kernel, planes),
        packs,
        [
            ((RING * TAP_ROWS, channels), BF16),
            ((channels, RING * TAP_ROWS), BF16),
            ((group, inner), F32),
            ((group, 2 * W), F32),
        ],
        [],
        PREPARE,
        RING * TAP_ROWS * WIDE * 4,
        "prepare",
    )
    own, low, high, up, down = call(
        functools.partial(forward_kernel, planes),
        (x, w, cot),
        [((group, inner), F32), plane, plane, edge, edge],
        [pltpu.VMEM((TAP_ROWS, outer), F32)] * RING,
        flops,
        2 * channels * outer,
        "conv_forward",
    )
    before = lax.ppermute(up, "space", [(i, i + 1) for i in range(slabs - 1)])
    after = lax.ppermute(down, "space", [(i + 1, i) for i in range(slabs - 1)])
    back = ((TAP_ROWS + 16 * planes, WIDE), BF16)
    part, *backs = call(
        functools.partial(backward_kernel, planes),
        (x, own, low, high, before, after, cot, bias, turned),
        [((channels, outer), BF16)] + [back] * RING,
        [pltpu.VMEM((TAP_ROWS, outer), F32)] * RING
        + [
            pltpu.VMEM((RING * TAP_ROWS, outer), BF16),
            pltpu.VMEM((channels, outer), BF16),
            pltpu.SemaphoreType.DMA((planes,)),
        ],
        2 * flops,
        4 * channels * outer,
        "conv_backward",
        (),
        (0,),
    )
    backs = to_ring(backs)
    got = lax.all_to_all(part.reshape(parts, block, outer), "filt", 0, 0, tiled=True)
    filt, activation = call(
        functools.partial(unpack_kernel, planes),
        (*backs,),
        [((TAP_ROWS, WIDE), BF16), ((block, voxels), BF16)],
        [],
        UNPACK,
        RING * TAP_ROWS * WIDE * 2,
        "unpack",
    )
    by = lambda m: [(i, i ^ m) for i in range(slabs)]
    other = lax.ppermute(filt, "space", by(1))
    filt = (filt.astype(F32) + other.astype(F32)).astype(BF16)
    other = lax.ppermute(filt, "space", by(2))
    input_grad, weight_grad = call(
        functools.partial(collect_kernel, planes, 1.0 / math.sqrt(planes * slabs * PLANE)),
        (got, filt, other),
        [((block, voxels), BF16), ((len(TAPS) * block, channels), F32)],
        [],
        0,
        2 * channels * outer,
        "collect",
    )
    weight_grad = weight_grad.reshape(len(TAPS), block, channels)
    shape = features.shape
    return (
        activation.reshape(shape),
        input_grad.reshape(shape),
        jnp.transpose(weight_grad, (1, 0, 2)),
    )


def solution(mesh):
    return jax.shard_map(
        per_device,
        mesh=mesh,
        in_specs=(
            P("filt", "space", None),
            P("filt", None, None),
            P("filt"),
            P("filt", "space", None),
        ),
        out_specs=(P("filt", "space", None), P("filt", "space", None), P("filt", None, None)),
        check_vma=False,
    )
```

```python
import functools
import math

import jax
import jax.numpy as jnp
from jax import lax
from jax.experimental import pallas as pl
from jax.experimental.pallas import tpu as pltpu
from jax.sharding import PartitionSpec as P

H = 32
W = 64
PLANE = H * W
TAPS = [(kd, kh, kw) for kd in (-1, 0, 1) for kh in (-1, 0, 1) for kw in (-1, 0, 1)]
RING = 4
ROWS = H // RING
INNER = ROWS * W
OUTER = INNER + 2 * W
BLOCK = 8
WIDE = 256
TAP_ROWS = 224
PACK = 0
PREPARE = 8 * 10**9
UNPACK = 16 * 10**9
F32 = jnp.float32
BF16 = jnp.bfloat16


def moved(x, shift):
    return pltpu.roll(x, shift % x.shape[-1], x.ndim - 1) if shift else x


def fold(x):
    return jnp.concatenate([x[:, :WIDE], x[:, WIDE:]], axis=0)


def unfold(x):
    return jnp.concatenate([x[:BLOCK], x[BLOCK:]], axis=1)


def inside_row(rows, kw):
    col = lax.broadcasted_iota(jnp.int32, (rows, OUTER), 1) % W
    return (col + kw >= 0) & (col + kw < W)


def hop(slot, core):
    return (0, 1 + 2 * core, 2, 3 - 2 * core)[slot]


def ring_chunk(slot):
    at = jnp.bitwise_and(lax.axis_index("filt"), RING - 1)
    core = jnp.bitwise_and(lax.axis_index("space"), 1)
    return jnp.bitwise_xor(at, hop(slot, core))


def swapped(x):
    return jnp.concatenate([x[slot * BLOCK : (slot + 1) * BLOCK] for slot in (0, 3, 2, 1)], 0)


def pack_kernel(planes, x_any, cot_any, bias_any, chunks, *refs):
    packs, (x_ref, cot_ref, bias_ref, in_sems) = refs[:RING], refs[RING:]
    copies = [
        pltpu.make_async_copy(src, dst, in_sems.at[i])
        for i, (src, dst) in enumerate(((x_any, x_ref), (cot_any, cot_ref), (bias_any, bias_ref)))
    ]
    for copy in copies:
        copy.start()
    copies[0].wait()
    lane = lax.broadcasted_iota(jnp.int32, (BLOCK, 2 * W), 1)
    for v in range(RING):
        for d in range(planes):
            base = d * PLANE + v * INNER
            halo = jnp.zeros((BLOCK, 2 * W), F32)
            if v < RING - 1:
                below = x_ref[:, base + INNER : base + INNER + 2 * W].astype(F32)
                halo = jnp.where(lane < W, below, halo)
            if v > 0:
                above = x_ref[:, base - 2 * W : base].astype(F32)
                halo = jnp.where(lane < W, halo, above)
            own, halo = x_ref[:, base : base + INNER], halo.astype(BF16)
            for g in range(chunks.shape[0] // RING):
                chunks[g * RING + v, :, d * OUTER : d * OUTER + INNER] = own
                chunks[g * RING + v, :, d * OUTER + INNER : (d + 1) * OUTER] = halo
    copies[1].wait()
    copies[2].wait()
    bias = jnp.broadcast_to(bias_ref[...].astype(F32), (16, BLOCK))
    bias = jnp.concatenate([bias, jnp.zeros((16, WIDE - BLOCK), F32)], 1).astype(BF16)
    for slot, pack in enumerate(packs):
        for d in range(planes):
            start = ring_chunk(slot) * INNER + d * PLANE
            rows = cot_ref[:, pl.ds(pl.multiple_of(start, INNER), INNER)]
            pack[16 * d : 16 * d + 16, :] = fold(rows.astype(F32)).astype(BF16)
        pack[16 * planes : 16 * planes + 16, :] = bias


def upstream(packs, d):
    rows = slice(16 * d, 16 * d + 16)
    return jnp.concatenate([unfold(pack[rows, :].astype(F32)) for pack in packs], 0)


def offsets(packs, planes):
    diagonal = lax.broadcasted_iota(jnp.int32, (BLOCK, 2 * W), 0) == lax.broadcasted_iota(
        jnp.int32, (BLOCK, 2 * W), 1
    )
    rows = slice(16 * planes, 16 * planes + 16)
    columns = []
    for pack in packs:
        row = pack[rows, 0 : 2 * W].astype(F32)[:BLOCK]
        columns.append(jnp.sum(jnp.where(diagonal, row, 0.0), axis=1, keepdims=True))
    return jnp.concatenate(columns, 0)


def prepare_kernel(*refs):
    taps, (w_ref, turned_ref) = refs[:RING], refs[RING:]
    for m in range(RING):
        w = jnp.concatenate([taps[m][...].astype(F32), jnp.zeros((BLOCK, WIDE), F32)], 0)
        w_ref[m * TAP_ROWS : (m + 1) * TAP_ROWS, :] = w.astype(BF16)
    turned_ref[...] = w_ref[...].T


def forward_kernel(
    planes, x_ref, w_ref, *refs
):
    packs, (own_ref, low_ref, high_ref, up_ref, down_ref) = refs[:RING], refs[RING : RING + 5]
    maps = refs[RING + 5 :]
    for m in range(RING):
        w = w_ref[m * TAP_ROWS : (m + 1) * TAP_ROWS, :]
        maps[m][...] = jnp.dot(w, x_ref[...], preferred_element_type=F32)
    masks = {kw: inside_row(BLOCK, kw) for kw in (-1, 1)}
    for out in range(-1, planes + 1):
        pieces = []
        for m in range(RING):
            total = None
            for kh in (-1, 0, 1):
                line = None
                for kw in (-1, 0, 1):
                    term = None
                    for kd in (-1, 0, 1):
                        if 0 <= out + kd < planes:
                            at = TAPS.index((kd, kh, kw)) * BLOCK
                            d = out + kd
                            part = maps[m][at : at + BLOCK, d * OUTER : (d + 1) * OUTER]
                            term = part if term is None else term + part
                    if kw:
                        term = jnp.where(masks[kw], moved(term, -kw), 0.0)
                    line = term if line is None else line + term
                line = moved(line, -kh * W)
                total = line if total is None else total + line
            pieces.append(total[:, :INNER])
        total = jnp.concatenate(pieces, 0)
        if out < 0:
            low_ref[...] = total
            down_ref[:, 0:INNER] = total.astype(BF16)
        elif out >= planes:
            high_ref[...] = total
            up_ref[:, 0:INNER] = total.astype(BF16)
        else:
            own_ref[:, out * INNER : (out + 1) * INNER] = total
        for edge, ref in ((planes - 1, up_ref), (0, down_ref)):
            if out == edge:
                ref[:, INNER : 2 * INNER] = total.astype(BF16)
                ref[:, 2 * INNER : 3 * INNER] = upstream(packs, out).astype(BF16)


def backward_kernel(
    planes, x_ref, own_ref, low_ref, high_ref, before_ref, after_ref, turned_ref, *refs
):
    packs, part_any, backs = refs[:RING], refs[RING], refs[RING + 1 : 2 * RING + 1]
    bank, (shifted, part, sems) = refs[2 * RING + 1 : 3 * RING + 1], refs[3 * RING + 1 :]
    bias = offsets(packs, planes)
    masks = {kw: inside_row(BLOCK, kw) for kw in (-1, 1)}
    for m in range(RING):
        bank[m][TAP_ROWS - BLOCK : TAP_ROWS, :] = jnp.zeros((BLOCK, planes * OUTER), F32)
    for src in range(-1, planes + 1):
        if src < 0:
            pre = swapped(before_ref[:, INNER : 2 * INNER].astype(F32)) + low_ref[...]
            cot = swapped(before_ref[:, 2 * INNER : 3 * INNER].astype(F32))
        elif src >= planes:
            pre = swapped(after_ref[:, INNER : 2 * INNER].astype(F32)) + high_ref[...]
            cot = swapped(after_ref[:, 2 * INNER : 3 * INNER].astype(F32))
        else:
            pre = own_ref[:, src * INNER : (src + 1) * INNER]
            cot = upstream(packs, src)
            if src == 0:
                pre = pre + swapped(before_ref[:, 0:INNER].astype(F32))
            if src == planes - 1:
                pre = pre + swapped(after_ref[:, 0:INNER].astype(F32))
        pre = pre + bias
        s = jax.nn.sigmoid(pre)
        if 0 <= src < planes:
            act = pre * s
            at = TAP_ROWS + 16 * src
            for m in range(RING):
                rows = act[m * BLOCK : (m + 1) * BLOCK]
                backs[m][at : at + 16, :] = fold(rows).astype(BF16)
        grad = (cot * (s * (1.0 + pre * (1.0 - s)))).astype(BF16).astype(F32)
        grad = jnp.concatenate([grad, jnp.zeros((grad.shape[0], 2 * W), F32)], 1)
        for m in range(RING):
            own = grad[m * BLOCK : (m + 1) * BLOCK]
            for kh in (-1, 0, 1):
                line = moved(own, kh * W)
                for kw in (-1, 0, 1):
                    term = line
                    if kw:
                        term = jnp.where(masks[-kw], moved(line, kw), 0.0)
                    for kd in (-1, 0, 1):
                        d = src + kd
                        if 0 <= d < planes:
                            at = TAPS.index((kd, kh, kw)) * BLOCK
                            bank[m][at : at + BLOCK, d * OUTER : (d + 1) * OUTER] = term
    for m in range(RING):
        rows = slice(m * TAP_ROWS, (m + 1) * TAP_ROWS)
        shifted[rows, :] = bank[m][...].astype(BF16)
        filt = lax.dot_general(
            shifted[rows, :], x_ref[...], (((1,), (1,)), ((), ())), preferred_element_type=F32
        )
        backs[m][0:TAP_ROWS, :] = filt.astype(BF16)
    copies = []
    for d in range(planes):
        lanes = slice(d * OUTER, (d + 1) * OUTER)
        total = jnp.dot(turned_ref[...], shifted[:, lanes], preferred_element_type=F32)
        part[:, lanes] = total.astype(BF16)
        copies.append(pltpu.make_async_copy(part.at[:, lanes], part_any.at[:, lanes], sems.at[d]))
        copies[-1].start()
    for copy in copies:
        copy.wait()


def unpack_kernel(planes, *refs):
    backs, (filt_ref, act_ref) = refs[:RING], refs[RING:]
    total = None
    for m, back in enumerate(backs):
        part = back[0:TAP_ROWS, :].astype(F32)
        total = part if total is None else total + part
        chunk = ring_chunk(m)
        for d in range(planes):
            lanes = pl.ds(pl.multiple_of(chunk * INNER + d * PLANE, INNER), INNER)
            start = TAP_ROWS + 16 * d
            act_ref[:, lanes] = unfold(back[start : start + 16, :].astype(F32)).astype(BF16)
    filt_ref[...] = total.astype(BF16)


def collect_kernel(planes, scale, got_ref, filt_ref, other_ref, out_ref, weight_ref):
    rows = weight_ref.shape[0]
    filt = filt_ref[...].astype(F32) + other_ref[...].astype(F32)
    weight_ref[...] = (filt * scale)[:rows]
    lane = lax.broadcasted_iota(jnp.int32, (BLOCK, 2 * W), 1)
    for d in range(planes):
        sums = []
        for v in range(RING):
            total = None
            for g in range(got_ref.shape[0] // RING):
                part = got_ref[g * RING + v, :, d * OUTER : (d + 1) * OUTER].astype(F32)
                total = part if total is None else total + part
            sums.append(total)
        for v in range(RING):
            first, last = sums[v][:, : 2 * W], sums[v][:, INNER - 2 * W : INNER]
            if v > 0:
                first = first + jnp.where(lane < W, sums[v - 1][:, INNER:], 0.0)
            if v < RING - 1:
                last = last + jnp.where(lane < W, 0.0, sums[v + 1][:, INNER:])
            whole = jnp.concatenate([first, sums[v][:, 2 * W : INNER - 2 * W], last], 1)
            base = d * PLANE + v * INNER
            out_ref[:, base : base + INNER] = whole.astype(BF16)


def call(kernel, ins, outs, scratch, flops, moved_bytes, name, hbm=(), outs_hbm=(), limit=48):
    smem = pl.BlockSpec(memory_space=pltpu.SMEM)
    vmem = pl.BlockSpec(memory_space=pltpu.VMEM)
    anywhere = pl.BlockSpec(memory_space=pl.ANY)
    shapes = tuple(jax.ShapeDtypeStruct(shape, kind) for shape, kind in outs)
    return pl.pallas_call(
        kernel,
        out_shape=shapes,
        in_specs=[smem if x.dtype == jnp.int32 else anywhere if i in hbm else vmem for i, x in enumerate(ins)],
        out_specs=tuple(anywhere if i in outs_hbm else vmem for i in range(len(outs))),
        scratch_shapes=scratch,
        compiler_params=pltpu.CompilerParams(vmem_limit_bytes=limit * 2**20),
        cost_estimate=pl.CostEstimate(flops=flops, bytes_accessed=moved_bytes, transcendentals=0),
        name=name,
    )(*ins)


def per_device(features, weight, bias_vec, cotangent):
    block, planes, _ = features.shape
    channels = weight.shape[2]
    parts = lax.axis_size("filt")
    slabs = lax.axis_size("space")
    voxels = planes * PLANE
    outer = planes * OUTER
    inner = planes * INNER
    group = RING * BLOCK
    w = jnp.transpose(weight, (1, 0, 2)).reshape(len(TAPS) * block, channels)

    def to_slot(value, slot):
        pairs = [
            (s * parts + f, s * parts + (f ^ hop(slot, s & 1)))
            for s in range(slabs)
            for f in range(parts)
        ]
        return lax.ppermute(value, ("space", "filt"), pairs) if slot else value

    first, second = to_slot(w, 1), to_slot(w, 2)
    pack = ((16 * planes + 16, WIDE), BF16)
    chunks, *packs = call(
        functools.partial(pack_kernel, planes),
        (features.reshape(block, voxels), cotangent.reshape(block, voxels), bias_vec[None]),
        [((parts, block, outer), BF16)] + [pack] * RING,
        [
            pltpu.VMEM((block, voxels), BF16),
            pltpu.VMEM((block, voxels), BF16),
            pltpu.VMEM((1, block), BF16),
            pltpu.SemaphoreType.DMA((3,)),
        ],
        PACK,
        2 * parts * block * outer,
        "pack",
        (0, 1, 2),
        (),
        61,
    )
    packs = [to_slot(value, slot) for slot, value in enumerate(packs)]
    third = lax.ppermute(first, "space", [(s, s ^ 1) for s in range(slabs)])
    x = lax.all_to_all(chunks, "filt", 0, 0, tiled=True).reshape(channels, outer)

    edge = ((group, 3 * INNER), BF16)
    plane = ((group, INNER), F32)
    flops = 2 * RING * TAP_ROWS * channels * outer
    w, turned = call(
        prepare_kernel,
        (w, first, second, third),
        [((RING * TAP_ROWS, channels), BF16), ((channels, RING * TAP_ROWS), BF16)],
        [],
        PREPARE,
        RING * TAP_ROWS * WIDE * 4,
        "prepare",
    )
    own, low, high, up, down = call(
        functools.partial(forward_kernel, planes),
        (x, w, *packs),
        [((group, inner), F32), plane, plane, edge, edge],
        [pltpu.VMEM((TAP_ROWS, outer), F32)] * RING,
        flops,
        2 * channels * outer,
        "conv_forward",
    )
    before = lax.ppermute(up, "space", [(i, i + 1) for i in range(slabs - 1)])
    after = lax.ppermute(down, "space", [(i + 1, i) for i in range(slabs - 1)])
    back = ((TAP_ROWS + 16 * planes, WIDE), BF16)
    part, *backs = call(
        functools.partial(backward_kernel, planes),
        (x, own, low, high, before, after, turned, *packs),
        [((channels, outer), BF16)] + [back] * RING,
        [pltpu.VMEM((TAP_ROWS, outer), F32)] * RING
        + [
            pltpu.VMEM((RING * TAP_ROWS, outer), BF16),
            pltpu.VMEM((channels, outer), BF16),
            pltpu.SemaphoreType.DMA((planes,)),
        ],
        2 * flops,
        4 * channels * outer,
        "conv_backward",
        (),
        (0,),
    )
    backs = [to_slot(value, slot) for slot, value in enumerate(backs)]
    got = lax.all_to_all(part.reshape(parts, block, outer), "filt", 0, 0, tiled=True)
    filt, activation = call(
        functools.partial(unpack_kernel, planes),
        (*backs,),
        [((TAP_ROWS, WIDE), BF16), ((block, voxels), BF16)],
        [],
        UNPACK,
        RING * TAP_ROWS * WIDE * 2,
        "unpack",
    )
    by = lambda m: [(i, i ^ m) for i in range(slabs)]
    other = lax.ppermute(filt, "space", by(1))
    filt = (filt.astype(F32) + other.astype(F32)).astype(BF16)
    other = lax.ppermute(filt, "space", by(2))
    input_grad, weight_grad = call(
        functools.partial(collect_kernel, planes, 1.0 / math.sqrt(planes * slabs * PLANE)),
        (got, filt, other),
        [((block, voxels), BF16), ((len(TAPS) * block, channels), F32)],
        [],
        0,
        2 * channels * outer,
        "collect",
    )
    weight_grad = weight_grad.reshape(len(TAPS), block, channels)
    shape = features.shape
    return (
        activation.reshape(shape),
        input_grad.reshape(shape),
        jnp.transpose(weight_grad, (1, 0, 2)),
    )


def solution(mesh):
    return jax.shard_map(
        per_device,
        mesh=mesh,
        in_specs=(
            P("filt", "space", None),
            P("filt", None, None),
            P("filt"),
            P("filt", "space", None),
        ),
        out_specs=(P("filt", "space", None), P("filt", "space", None), P("filt", None, None)),
        check_vma=False,
    )
```

```python
import functools
import math

import jax
import jax.numpy as jnp
from jax import lax
from jax.experimental import pallas as pl
from jax.experimental.pallas import tpu as pltpu
from jax.sharding import PartitionSpec as P

H = 32
W = 64
PLANE = H * W
TAPS = [(kd, kh, kw) for kd in (-1, 0, 1) for kh in (-1, 0, 1) for kw in (-1, 0, 1)]
RING = 4
ROWS = H // RING
INNER = ROWS * W
OUTER = INNER + 2 * W
BLOCK = 8
WIDE = 256
TAP_ROWS = 224
PACK = 0
PREPARE = 8 * 10**9
UNPACK = 16 * 10**9
F32 = jnp.float32
BF16 = jnp.bfloat16


def moved(x, shift):
    return pltpu.roll(x, shift % x.shape[-1], x.ndim - 1) if shift else x


def fold(x):
    return jnp.concatenate([x[:, :WIDE], x[:, WIDE:]], axis=0)


def unfold(x):
    return jnp.concatenate([x[:BLOCK], x[BLOCK:]], axis=1)


def inside_row(rows, kw):
    col = lax.broadcasted_iota(jnp.int32, (rows, OUTER), 1) % W
    return (col + kw >= 0) & (col + kw < W)


def hop(slot, core):
    return (0, 1 + 2 * core, 2, 3 - 2 * core)[slot]


def ring_chunk(slot):
    at = jnp.bitwise_and(lax.axis_index("filt"), RING - 1)
    core = jnp.bitwise_and(lax.axis_index("space"), 1)
    return jnp.bitwise_xor(at, hop(slot, core))


def swapped(x):
    return jnp.concatenate([x[slot * BLOCK : (slot + 1) * BLOCK] for slot in (0, 3, 2, 1)], 0)


def pack_kernel(planes, x_any, cot_any, bias_any, chunks, *refs):
    packs, (x_ref, cot_ref, bias_ref, in_sems) = refs[:RING], refs[RING:]
    copies = [
        pltpu.make_async_copy(src, dst, in_sems.at[i])
        for i, (src, dst) in enumerate(((x_any, x_ref), (cot_any, cot_ref), (bias_any, bias_ref)))
    ]
    for copy in copies:
        copy.start()
    copies[0].wait()
    lane = lax.broadcasted_iota(jnp.int32, (BLOCK, 2 * W), 1)
    for v in range(RING):
        for d in range(planes):
            base = d * PLANE + v * INNER
            halo = jnp.zeros((BLOCK, 2 * W), F32)
            if v < RING - 1:
                below = x_ref[:, base + INNER : base + INNER + 2 * W].astype(F32)
                halo = jnp.where(lane < W, below, halo)
            if v > 0:
                above = x_ref[:, base - 2 * W : base].astype(F32)
                halo = jnp.where(lane < W, halo, above)
            own, halo = x_ref[:, base : base + INNER], halo.astype(BF16)
            for g in range(chunks.shape[0] // RING):
                chunks[g * RING + v, :, d * OUTER : d * OUTER + INNER] = own
                chunks[g * RING + v, :, d * OUTER + INNER : (d + 1) * OUTER] = halo
    copies[1].wait()
    copies[2].wait()
    bias = jnp.broadcast_to(bias_ref[...].astype(F32), (16, BLOCK))
    bias = jnp.concatenate([bias, jnp.zeros((16, WIDE - BLOCK), F32)], 1).astype(BF16)
    for slot, pack in enumerate(packs):
        for d in range(planes):
            start = ring_chunk(slot) * INNER + d * PLANE
            rows = cot_ref[:, pl.ds(pl.multiple_of(start, INNER), INNER)]
            pack[16 * d : 16 * d + 16, :] = fold(rows.astype(F32)).astype(BF16)
        pack[16 * planes : 16 * planes + 16, :] = bias


def odd_slab():
    return jnp.bitwise_and(lax.axis_index("space"), 1) == 1


def upstream(packs, d):
    rows = slice(16 * d, 16 * d + 16)
    return jnp.concatenate([unfold(pack[rows, :].astype(F32)) for pack in packs], 0)


def offsets(packs, planes):
    diagonal = lax.broadcasted_iota(jnp.int32, (BLOCK, 2 * W), 0) == lax.broadcasted_iota(
        jnp.int32, (BLOCK, 2 * W), 1
    )
    rows = slice(16 * planes, 16 * planes + 16)
    columns = []
    for pack in packs:
        row = pack[rows, 0 : 2 * W].astype(F32)[:BLOCK]
        columns.append(jnp.sum(jnp.where(diagonal, row, 0.0), axis=1, keepdims=True))
    return jnp.concatenate(columns, 0)


def prepare_kernel(*refs):
    taps, (w_ref, turned_ref) = refs[:RING], refs[RING:]
    for m in range(RING):
        w = jnp.concatenate([taps[m][...].astype(F32), jnp.zeros((BLOCK, WIDE), F32)], 0)
        w_ref[m * TAP_ROWS : (m + 1) * TAP_ROWS, :] = w.astype(BF16)
    turned_ref[...] = w_ref[...].T


def forward_kernel(
    planes, x_ref, w_ref, *refs
):
    packs, (own_ref, low_ref, high_ref, far_ref, near_ref) = refs[:RING], refs[RING : RING + 5]
    maps, edges = refs[RING + 5 : 2 * RING + 5], refs[2 * RING + 5 :]
    down_ref, up_ref = edges
    for m in range(RING):
        w = w_ref[m * TAP_ROWS : (m + 1) * TAP_ROWS, :]
        maps[m][...] = jnp.dot(w, x_ref[...], preferred_element_type=F32)
    masks = {kw: inside_row(BLOCK, kw) for kw in (-1, 1)}
    for out in range(-1, planes + 1):
        pieces = []
        for m in range(RING):
            total = None
            for kh in (-1, 0, 1):
                line = None
                for kw in (-1, 0, 1):
                    term = None
                    for kd in (-1, 0, 1):
                        if 0 <= out + kd < planes:
                            at = TAPS.index((kd, kh, kw)) * BLOCK
                            d = out + kd
                            part = maps[m][at : at + BLOCK, d * OUTER : (d + 1) * OUTER]
                            term = part if term is None else term + part
                    if kw:
                        term = jnp.where(masks[kw], moved(term, -kw), 0.0)
                    line = term if line is None else line + term
                line = moved(line, -kh * W)
                total = line if total is None else total + line
            pieces.append(total[:, :INNER])
        total = jnp.concatenate(pieces, 0)
        if out < 0:
            low_ref[...] = total
            down_ref[:, 0:INNER] = total
        elif out >= planes:
            high_ref[...] = total
            up_ref[:, 0:INNER] = total
        else:
            own_ref[:, out * INNER : (out + 1) * INNER] = total
        for edge, ref in ((planes - 1, up_ref), (0, down_ref)):
            if out == edge:
                ref[:, INNER : 2 * INNER] = total
                ref[:, 2 * INNER : 3 * INNER] = upstream(packs, out)
    down, up = down_ref[...], up_ref[...]
    near_ref[...] = jnp.where(odd_slab(), down, up).astype(BF16)
    far_ref[...] = jnp.where(odd_slab(), up, down).astype(BF16)


def backward_kernel(
    planes, x_ref, own_ref, low_ref, high_ref, far_ref, near_ref, turned_ref, *refs
):
    packs, part_any, backs = refs[:RING], refs[RING], refs[RING + 1 : 2 * RING + 1]
    bank, (shifted, part, sems) = refs[2 * RING + 1 : 3 * RING + 1], refs[3 * RING + 1 :]
    bias = offsets(packs, planes)
    near, far = swapped(near_ref[...].astype(F32)), swapped(far_ref[...].astype(F32))
    before, after = jnp.where(odd_slab(), near, far), jnp.where(odd_slab(), far, near)
    masks = {kw: inside_row(BLOCK, kw) for kw in (-1, 1)}
    for m in range(RING):
        bank[m][TAP_ROWS - BLOCK : TAP_ROWS, :] = jnp.zeros((BLOCK, planes * OUTER), F32)
    for src in range(-1, planes + 1):
        if src < 0:
            pre = before[:, INNER : 2 * INNER] + low_ref[...]
            cot = before[:, 2 * INNER : 3 * INNER]
        elif src >= planes:
            pre = after[:, INNER : 2 * INNER] + high_ref[...]
            cot = after[:, 2 * INNER : 3 * INNER]
        else:
            pre = own_ref[:, src * INNER : (src + 1) * INNER]
            cot = upstream(packs, src)
            if src == 0:
                pre = pre + before[:, 0:INNER]
            if src == planes - 1:
                pre = pre + after[:, 0:INNER]
        pre = pre + bias
        s = jax.nn.sigmoid(pre)
        if 0 <= src < planes:
            act = pre * s
            at = TAP_ROWS + 16 * src
            for m in range(RING):
                rows = act[m * BLOCK : (m + 1) * BLOCK]
                backs[m][at : at + 16, :] = fold(rows).astype(BF16)
        grad = (cot * (s * (1.0 + pre * (1.0 - s)))).astype(BF16).astype(F32)
        grad = jnp.concatenate([grad, jnp.zeros((grad.shape[0], 2 * W), F32)], 1)
        for m in range(RING):
            own = grad[m * BLOCK : (m + 1) * BLOCK]
            for kh in (-1, 0, 1):
                line = moved(own, kh * W)
                for kw in (-1, 0, 1):
                    term = line
                    if kw:
                        term = jnp.where(masks[-kw], moved(line, kw), 0.0)
                    for kd in (-1, 0, 1):
                        d = src + kd
                        if 0 <= d < planes:
                            at = TAPS.index((kd, kh, kw)) * BLOCK
                            bank[m][at : at + BLOCK, d * OUTER : (d + 1) * OUTER] = term
    for m in range(RING):
        rows = slice(m * TAP_ROWS, (m + 1) * TAP_ROWS)
        shifted[rows, :] = bank[m][...].astype(BF16)
        filt = lax.dot_general(
            shifted[rows, :], x_ref[...], (((1,), (1,)), ((), ())), preferred_element_type=F32
        )
        backs[m][0:TAP_ROWS, :] = filt.astype(BF16)
    copies = []
    for d in range(planes):
        lanes = slice(d * OUTER, (d + 1) * OUTER)
        total = jnp.dot(turned_ref[...], shifted[:, lanes], preferred_element_type=F32)
        part[:, lanes] = total.astype(BF16)
        copies.append(pltpu.make_async_copy(part.at[:, lanes], part_any.at[:, lanes], sems.at[d]))
        copies[-1].start()
    for copy in copies:
        copy.wait()


def unpack_kernel(planes, *refs):
    backs, (filt_ref, act_ref) = refs[:RING], refs[RING:]
    total = None
    for m, back in enumerate(backs):
        part = back[0:TAP_ROWS, :].astype(F32)
        total = part if total is None else total + part
        chunk = ring_chunk(m)
        for d in range(planes):
            lanes = pl.ds(pl.multiple_of(chunk * INNER + d * PLANE, INNER), INNER)
            start = TAP_ROWS + 16 * d
            act_ref[:, lanes] = unfold(back[start : start + 16, :].astype(F32)).astype(BF16)
    filt_ref[...] = total.astype(BF16)


def collect_kernel(planes, scale, got_ref, filt_ref, other_ref, out_ref, weight_ref):
    rows = weight_ref.shape[0]
    filt = filt_ref[...].astype(F32) + other_ref[...].astype(F32)
    weight_ref[...] = (filt * scale)[:rows]
    lane = lax.broadcasted_iota(jnp.int32, (BLOCK, 2 * W), 1)
    for d in range(planes):
        sums = []
        for v in range(RING):
            total = None
            for g in range(got_ref.shape[0] // RING):
                part = got_ref[g * RING + v, :, d * OUTER : (d + 1) * OUTER].astype(F32)
                total = part if total is None else total + part
            sums.append(total)
        for v in range(RING):
            first, last = sums[v][:, : 2 * W], sums[v][:, INNER - 2 * W : INNER]
            if v > 0:
                first = first + jnp.where(lane < W, sums[v - 1][:, INNER:], 0.0)
            if v < RING - 1:
                last = last + jnp.where(lane < W, 0.0, sums[v + 1][:, INNER:])
            whole = jnp.concatenate([first, sums[v][:, 2 * W : INNER - 2 * W], last], 1)
            base = d * PLANE + v * INNER
            out_ref[:, base : base + INNER] = whole.astype(BF16)


def call(kernel, ins, outs, scratch, flops, moved_bytes, name, hbm=(), outs_hbm=(), limit=48):
    smem = pl.BlockSpec(memory_space=pltpu.SMEM)
    vmem = pl.BlockSpec(memory_space=pltpu.VMEM)
    anywhere = pl.BlockSpec(memory_space=pl.ANY)
    shapes = tuple(jax.ShapeDtypeStruct(shape, kind) for shape, kind in outs)
    return pl.pallas_call(
        kernel,
        out_shape=shapes,
        in_specs=[smem if x.dtype == jnp.int32 else anywhere if i in hbm else vmem for i, x in enumerate(ins)],
        out_specs=tuple(anywhere if i in outs_hbm else vmem for i in range(len(outs))),
        scratch_shapes=scratch,
        compiler_params=pltpu.CompilerParams(vmem_limit_bytes=limit * 2**20),
        cost_estimate=pl.CostEstimate(flops=flops, bytes_accessed=moved_bytes, transcendentals=0),
        name=name,
    )(*ins)


def per_device(features, weight, bias_vec, cotangent):
    block, planes, _ = features.shape
    channels = weight.shape[2]
    parts = lax.axis_size("filt")
    slabs = lax.axis_size("space")
    voxels = planes * PLANE
    outer = planes * OUTER
    inner = planes * INNER
    group = RING * BLOCK
    w = jnp.transpose(weight, (1, 0, 2)).reshape(len(TAPS) * block, channels)

    def to_slot(value, slot):
        pairs = [
            (s * parts + f, s * parts + (f ^ hop(slot, s & 1)))
            for s in range(slabs)
            for f in range(parts)
        ]
        return lax.ppermute(value, ("space", "filt"), pairs) if slot else value

    first, second = to_slot(w, 1), to_slot(w, 2)
    pack = ((16 * planes + 16, WIDE), BF16)
    chunks, *packs = call(
        functools.partial(pack_kernel, planes),
        (features.reshape(block, voxels), cotangent.reshape(block, voxels), bias_vec[None]),
        [((parts, block, outer), BF16)] + [pack] * RING,
        [
            pltpu.VMEM((block, voxels), BF16),
            pltpu.VMEM((block, voxels), BF16),
            pltpu.VMEM((1, block), BF16),
            pltpu.SemaphoreType.DMA((3,)),
        ],
        PACK,
        2 * parts * block * outer,
        "pack",
        (0, 1, 2),
        (),
        61,
    )
    packs = [to_slot(value, slot) for slot, value in enumerate(packs)]
    third = lax.ppermute(first, "space", [(s, s ^ 1) for s in range(slabs)])
    x = lax.all_to_all(chunks, "filt", 0, 0, tiled=True).reshape(channels, outer)

    edge = ((group, 3 * INNER), BF16)
    plane = ((group, INNER), F32)
    flops = 2 * RING * TAP_ROWS * channels * outer
    w, turned = call(
        prepare_kernel,
        (w, first, second, third),
        [((RING * TAP_ROWS, channels), BF16), ((channels, RING * TAP_ROWS), BF16)],
        [],
        PREPARE,
        RING * TAP_ROWS * WIDE * 4,
        "prepare",
    )
    own, low, high, far, near = call(
        functools.partial(forward_kernel, planes),
        (x, w, *packs),
        [((group, inner), F32), plane, plane, edge, edge],
        [pltpu.VMEM((TAP_ROWS, outer), F32)] * RING + [pltpu.VMEM((group, 3 * INNER), F32)] * 2,
        flops,
        2 * channels * outer,
        "conv_forward",
    )
    inner_slabs = [(s, s + 1 - 2 * (1 - s % 2)) for s in range(1, slabs - 1)]
    far = lax.ppermute(far, "space", inner_slabs)
    near = lax.ppermute(near, "space", [(s, s ^ 1) for s in range(slabs)])
    back = ((TAP_ROWS + 16 * planes, WIDE), BF16)
    part, *backs = call(
        functools.partial(backward_kernel, planes),
        (x, own, low, high, far, near, turned, *packs),
        [((channels, outer), BF16)] + [back] * RING,
        [pltpu.VMEM((TAP_ROWS, outer), F32)] * RING
        + [
            pltpu.VMEM((RING * TAP_ROWS, outer), BF16),
            pltpu.VMEM((channels, outer), BF16),
            pltpu.SemaphoreType.DMA((planes,)),
        ],
        2 * flops,
        4 * channels * outer,
        "conv_backward",
        (),
        (0,),
    )
    backs = [to_slot(value, slot) for slot, value in enumerate(backs)]
    got = lax.all_to_all(part.reshape(parts, block, outer), "filt", 0, 0, tiled=True)
    filt, activation = call(
        functools.partial(unpack_kernel, planes),
        (*backs,),
        [((TAP_ROWS, WIDE), BF16), ((block, voxels), BF16)],
        [],
        UNPACK,
        RING * TAP_ROWS * WIDE * 2,
        "unpack",
    )
    by = lambda m: [(i, i ^ m) for i in range(slabs)]
    other = lax.ppermute(filt, "space", by(1))
    filt = (filt.astype(F32) + other.astype(F32)).astype(BF16)
    other = lax.ppermute(filt, "space", by(2))
    input_grad, weight_grad = call(
        functools.partial(collect_kernel, planes, 1.0 / math.sqrt(planes * slabs * PLANE)),
        (got, filt, other),
        [((block, voxels), BF16), ((len(TAPS) * block, channels), F32)],
        [],
        0,
        2 * channels * outer,
        "collect",
    )
    weight_grad = weight_grad.reshape(len(TAPS), block, channels)
    shape = features.shape
    return (
        activation.reshape(shape),
        input_grad.reshape(shape),
        jnp.transpose(weight_grad, (1, 0, 2)),
    )


def solution(mesh):
    return jax.shard_map(
        per_device,
        mesh=mesh,
        in_specs=(
            P("filt", "space", None),
            P("filt", None, None),
            P("filt"),
            P("filt", "space", None),
        ),
        out_specs=(P("filt", "space", None), P("filt", "space", None), P("filt", None, None)),
        check_vma=False,
    )
```

```python
import functools
import math

import jax
import jax.numpy as jnp
from jax import lax
from jax.experimental import pallas as pl
from jax.experimental.pallas import tpu as pltpu
from jax.sharding import PartitionSpec as P

H = 32
W = 64
PLANE = H * W
TAPS = [(kd, kh, kw) for kd in (-1, 0, 1) for kh in (-1, 0, 1) for kw in (-1, 0, 1)]
RING = 4
ROWS = H // RING
INNER = ROWS * W
OUTER = INNER + 2 * W
BLOCK = 8
GROUP = RING * BLOCK
WIDE = 256
TAP_ROWS = 224
PACK = 0
PREPARE = 8 * 10**9
UNPACK = 16 * 10**9
F32 = jnp.float32
BF16 = jnp.bfloat16


def moved(x, shift):
    return pltpu.roll(x, shift % x.shape[-1], x.ndim - 1) if shift else x


def fold(x):
    return jnp.concatenate([x[:, :WIDE], x[:, WIDE:]], axis=0)


def unfold(x):
    return jnp.concatenate([x[:BLOCK], x[BLOCK:]], axis=1)


def inside_row(rows, kw):
    col = lax.broadcasted_iota(jnp.int32, (rows, OUTER), 1) % W
    return (col + kw >= 0) & (col + kw < W)


def hop(slot, core):
    return (0, 1 + 2 * core, 2, 3 - 2 * core)[slot]


def ring_chunk(slot):
    at = jnp.bitwise_and(lax.axis_index("filt"), RING - 1)
    core = jnp.bitwise_and(lax.axis_index("space"), 1)
    return jnp.bitwise_xor(at, hop(slot, core))


def swapped(x):
    return jnp.concatenate([x[slot * BLOCK : (slot + 1) * BLOCK] for slot in (0, 3, 2, 1)], 0)


def pack_kernel(planes, x_any, cot_any, bias_any, chunks, *refs):
    packs, (x_ref, cot_ref, bias_ref, in_sems) = refs[:RING], refs[RING:]
    copies = [
        pltpu.make_async_copy(src, dst, in_sems.at[i])
        for i, (src, dst) in enumerate(((x_any, x_ref), (cot_any, cot_ref), (bias_any, bias_ref)))
    ]
    for copy in copies:
        copy.start()
    copies[0].wait()
    lane = lax.broadcasted_iota(jnp.int32, (BLOCK, 2 * W), 1)
    for v in range(RING):
        for d in range(planes):
            base = d * PLANE + v * INNER
            halo = jnp.zeros((BLOCK, 2 * W), F32)
            if v < RING - 1:
                below = x_ref[:, base + INNER : base + INNER + 2 * W].astype(F32)
                halo = jnp.where(lane < W, below, halo)
            if v > 0:
                above = x_ref[:, base - 2 * W : base].astype(F32)
                halo = jnp.where(lane < W, halo, above)
            own, halo = x_ref[:, base : base + INNER], halo.astype(BF16)
            for g in range(chunks.shape[0] // RING):
                chunks[g * RING + v, :, d * OUTER : d * OUTER + INNER] = own
                chunks[g * RING + v, :, d * OUTER + INNER : (d + 1) * OUTER] = halo
    copies[1].wait()
    copies[2].wait()
    bias = jnp.broadcast_to(bias_ref[...].astype(F32), (16, BLOCK))
    bias = jnp.concatenate([bias, jnp.zeros((16, WIDE - BLOCK), F32)], 1).astype(BF16)
    for slot, pack in enumerate(packs):
        for d in range(planes):
            start = ring_chunk(slot) * INNER + d * PLANE
            rows = cot_ref[:, pl.ds(pl.multiple_of(start, INNER), INNER)]
            pack[16 * d : 16 * d + 16, :] = fold(rows.astype(F32)).astype(BF16)
        pack[16 * planes : 16 * planes + 16, :] = bias


def odd_slab():
    return jnp.bitwise_and(lax.axis_index("space"), 1) == 1


def upstream(packs, d):
    rows = slice(16 * d, 16 * d + 16)
    return jnp.concatenate([unfold(pack[rows, :].astype(F32)) for pack in packs], 0)


def offsets(packs, planes):
    diagonal = lax.broadcasted_iota(jnp.int32, (BLOCK, 2 * W), 0) == lax.broadcasted_iota(
        jnp.int32, (BLOCK, 2 * W), 1
    )
    rows = slice(16 * planes, 16 * planes + 16)
    columns = []
    for pack in packs:
        row = pack[rows, 0 : 2 * W].astype(F32)[:BLOCK]
        columns.append(jnp.sum(jnp.where(diagonal, row, 0.0), axis=1, keepdims=True))
    return jnp.concatenate(columns, 0)


def prepare_kernel(*refs):
    taps, (w_ref, turned_ref) = refs[:RING], refs[RING:]
    w = [ref[...].astype(F32) for ref in taps]
    for t in range(len(TAPS)):
        rows = [x[t * BLOCK : (t + 1) * BLOCK] for x in w]
        w_ref[t * GROUP : (t + 1) * GROUP, :] = jnp.concatenate(rows, 0).astype(BF16)
    end = len(TAPS) * GROUP
    w_ref[end:, :] = jnp.zeros((w_ref.shape[0] - end, WIDE), BF16)
    turned_ref[...] = w_ref[...].T


def forward_kernel(planes, x_ref, w_ref, *refs):
    packs, (own_ref, low_ref, high_ref, far_ref, near_ref) = refs[:RING], refs[RING : RING + 5]
    maps, down_ref, up_ref = refs[RING + 5 :]
    maps[...] = jnp.dot(w_ref[...], x_ref[...], preferred_element_type=F32)
    masks = {kw: inside_row(GROUP, kw) for kw in (-1, 1)}
    for out in range(-1, planes + 1):
        total = None
        for kh in (-1, 0, 1):
            line = None
            for kw in (-1, 0, 1):
                term = None
                for kd in (-1, 0, 1):
                    d = out + kd
                    if 0 <= d < planes:
                        at = TAPS.index((kd, kh, kw)) * GROUP
                        part = maps[at : at + GROUP, d * OUTER : (d + 1) * OUTER]
                        term = part if term is None else term + part
                if kw:
                    term = jnp.where(masks[kw], moved(term, -kw), 0.0)
                line = term if line is None else line + term
            line = moved(line, -kh * W)
            total = line if total is None else total + line
        total = total[:, :INNER]
        if out < 0:
            low_ref[...] = total
            down_ref[:, 0:INNER] = total
        elif out >= planes:
            high_ref[...] = total
            up_ref[:, 0:INNER] = total
        else:
            own_ref[:, out * INNER : (out + 1) * INNER] = total
        for edge, ref in ((planes - 1, up_ref), (0, down_ref)):
            if out == edge:
                ref[:, INNER : 2 * INNER] = total
                ref[:, 2 * INNER : 3 * INNER] = upstream(packs, out)
    down, up = down_ref[...], up_ref[...]
    near_ref[...] = jnp.where(odd_slab(), down, up).astype(BF16)
    far_ref[...] = jnp.where(odd_slab(), up, down).astype(BF16)


def backward_kernel(
    planes, x_ref, own_ref, low_ref, high_ref, far_ref, near_ref, turned_ref, *refs
):
    packs, part_any, backs = refs[:RING], refs[RING], refs[RING + 1 : 2 * RING + 1]
    shifted, part, sems = refs[2 * RING + 1 :]
    bias = offsets(packs, planes)
    near, far = swapped(near_ref[...].astype(F32)), swapped(far_ref[...].astype(F32))
    before, after = jnp.where(odd_slab(), near, far), jnp.where(odd_slab(), far, near)
    masks = {kw: inside_row(GROUP, kw) for kw in (-1, 1)}
    end = len(TAPS) * GROUP
    shifted[end:, :] = jnp.zeros((shifted.shape[0] - end, planes * OUTER), BF16)
    for src in range(-1, planes + 1):
        if src < 0:
            pre = before[:, INNER : 2 * INNER] + low_ref[...]
            cot = before[:, 2 * INNER : 3 * INNER]
        elif src >= planes:
            pre = after[:, INNER : 2 * INNER] + high_ref[...]
            cot = after[:, 2 * INNER : 3 * INNER]
        else:
            pre = own_ref[:, src * INNER : (src + 1) * INNER]
            cot = upstream(packs, src)
            if src == 0:
                pre = pre + before[:, 0:INNER]
            if src == planes - 1:
                pre = pre + after[:, 0:INNER]
        pre = pre + bias
        s = jax.nn.sigmoid(pre)
        if 0 <= src < planes:
            act = pre * s
            at = TAP_ROWS + 16 * src
            for m in range(RING):
                rows = act[m * BLOCK : (m + 1) * BLOCK]
                backs[m][at : at + 16, :] = fold(rows).astype(BF16)
        grad = (cot * (s * (1.0 + pre * (1.0 - s)))).astype(BF16).astype(F32)
        grad = jnp.concatenate([grad, jnp.zeros((grad.shape[0], 2 * W), F32)], 1)
        for kh in (-1, 0, 1):
            line = moved(grad, kh * W)
            for kw in (-1, 0, 1):
                term = line
                if kw:
                    term = jnp.where(masks[-kw], moved(line, kw), 0.0)
                term = term.astype(BF16)
                for kd in (-1, 0, 1):
                    d = src + kd
                    if 0 <= d < planes:
                        at = TAPS.index((kd, kh, kw)) * GROUP
                        shifted[at : at + GROUP, d * OUTER : (d + 1) * OUTER] = term
    copies = []
    for d in range(planes):
        lanes = slice(d * OUTER, (d + 1) * OUTER)
        total = jnp.dot(turned_ref[...], shifted[:, lanes], preferred_element_type=F32)
        part[:, lanes] = total.astype(BF16)
        copies.append(pltpu.make_async_copy(part.at[:, lanes], part_any.at[:, lanes], sems.at[d]))
        copies[-1].start()
    filt = lax.dot_general(
        shifted[...], x_ref[...], (((1,), (1,)), ((), ())), preferred_element_type=F32
    )
    for m in range(RING):
        rows = [t * GROUP + m * BLOCK for t in range(len(TAPS))]
        pieces = [filt[at : at + BLOCK] for at in rows] + [jnp.zeros((BLOCK, WIDE), F32)]
        backs[m][0:TAP_ROWS, :] = jnp.concatenate(pieces, 0).astype(BF16)
    for copy in copies:
        copy.wait()


def unpack_kernel(planes, *refs):
    backs, (filt_ref, act_ref) = refs[:RING], refs[RING:]
    total = None
    for m, back in enumerate(backs):
        part = back[0:TAP_ROWS, :].astype(F32)
        total = part if total is None else total + part
        chunk = ring_chunk(m)
        for d in range(planes):
            lanes = pl.ds(pl.multiple_of(chunk * INNER + d * PLANE, INNER), INNER)
            start = TAP_ROWS + 16 * d
            act_ref[:, lanes] = unfold(back[start : start + 16, :].astype(F32)).astype(BF16)
    filt_ref[...] = total.astype(BF16)


def collect_kernel(planes, scale, got_ref, filt_ref, other_ref, out_ref, weight_ref):
    rows = weight_ref.shape[0]
    filt = filt_ref[...].astype(F32) + other_ref[...].astype(F32)
    weight_ref[...] = (filt * scale)[:rows]
    lane = lax.broadcasted_iota(jnp.int32, (BLOCK, 2 * W), 1)
    for d in range(planes):
        sums = []
        for v in range(RING):
            total = None
            for g in range(got_ref.shape[0] // RING):
                part = got_ref[g * RING + v, :, d * OUTER : (d + 1) * OUTER].astype(F32)
                total = part if total is None else total + part
            sums.append(total)
        for v in range(RING):
            first, last = sums[v][:, : 2 * W], sums[v][:, INNER - 2 * W : INNER]
            if v > 0:
                first = first + jnp.where(lane < W, sums[v - 1][:, INNER:], 0.0)
            if v < RING - 1:
                last = last + jnp.where(lane < W, 0.0, sums[v + 1][:, INNER:])
            whole = jnp.concatenate([first, sums[v][:, 2 * W : INNER - 2 * W], last], 1)
            base = d * PLANE + v * INNER
            out_ref[:, base : base + INNER] = whole.astype(BF16)


def call(kernel, ins, outs, scratch, flops, moved_bytes, name, hbm=(), outs_hbm=(), limit=48):
    smem = pl.BlockSpec(memory_space=pltpu.SMEM)
    vmem = pl.BlockSpec(memory_space=pltpu.VMEM)
    anywhere = pl.BlockSpec(memory_space=pl.ANY)
    shapes = tuple(jax.ShapeDtypeStruct(shape, kind) for shape, kind in outs)
    return pl.pallas_call(
        kernel,
        out_shape=shapes,
        in_specs=[smem if x.dtype == jnp.int32 else anywhere if i in hbm else vmem for i, x in enumerate(ins)],
        out_specs=tuple(anywhere if i in outs_hbm else vmem for i in range(len(outs))),
        scratch_shapes=scratch,
        compiler_params=pltpu.CompilerParams(vmem_limit_bytes=limit * 2**20),
        cost_estimate=pl.CostEstimate(flops=flops, bytes_accessed=moved_bytes, transcendentals=0),
        name=name,
    )(*ins)


def per_device(features, weight, bias_vec, cotangent):
    block, planes, _ = features.shape
    channels = weight.shape[2]
    parts = lax.axis_size("filt")
    slabs = lax.axis_size("space")
    voxels = planes * PLANE
    outer = planes * OUTER
    inner = planes * INNER
    group = RING * BLOCK
    w = jnp.transpose(weight, (1, 0, 2)).reshape(len(TAPS) * block, channels)

    def to_slot(value, slot):
        pairs = [
            (s * parts + f, s * parts + (f ^ hop(slot, s & 1)))
            for s in range(slabs)
            for f in range(parts)
        ]
        return lax.ppermute(value, ("space", "filt"), pairs) if slot else value

    first, second = to_slot(w, 1), to_slot(w, 2)
    pack = ((16 * planes + 16, WIDE), BF16)
    chunks, *packs = call(
        functools.partial(pack_kernel, planes),
        (features.reshape(block, voxels), cotangent.reshape(block, voxels), bias_vec[None]),
        [((parts, block, outer), BF16)] + [pack] * RING,
        [
            pltpu.VMEM((block, voxels), BF16),
            pltpu.VMEM((block, voxels), BF16),
            pltpu.VMEM((1, block), BF16),
            pltpu.SemaphoreType.DMA((3,)),
        ],
        PACK,
        2 * parts * block * outer,
        "pack",
        (0, 1, 2),
        (),
        61,
    )
    packs = [to_slot(value, slot) for slot, value in enumerate(packs)]
    third = lax.ppermute(first, "space", [(s, s ^ 1) for s in range(slabs)])
    x = lax.all_to_all(chunks, "filt", 0, 0, tiled=True).reshape(channels, outer)

    edge = ((group, 3 * INNER), BF16)
    plane = ((group, INNER), F32)
    flops = 2 * RING * TAP_ROWS * channels * outer
    w, turned = call(
        prepare_kernel,
        (w, first, second, third),
        [((RING * TAP_ROWS, channels), BF16), ((channels, RING * TAP_ROWS), BF16)],
        [],
        PREPARE,
        RING * TAP_ROWS * WIDE * 4,
        "prepare",
    )
    own, low, high, far, near = call(
        functools.partial(forward_kernel, planes),
        (x, w, *packs),
        [((group, inner), F32), plane, plane, edge, edge],
        [pltpu.VMEM((RING * TAP_ROWS, outer), F32)] + [pltpu.VMEM((group, 3 * INNER), F32)] * 2,
        flops,
        2 * channels * outer,
        "conv_forward",
    )
    inner_slabs = [(s, s + 1 - 2 * (1 - s % 2)) for s in range(1, slabs - 1)]
    far = lax.ppermute(far, "space", inner_slabs)
    near = lax.ppermute(near, "space", [(s, s ^ 1) for s in range(slabs)])
    back = ((TAP_ROWS + 16 * planes, WIDE), BF16)
    part, *backs = call(
        functools.partial(backward_kernel, planes),
        (x, own, low, high, far, near, turned, *packs),
        [((channels, outer), BF16)] + [back] * RING,
        [
            pltpu.VMEM((RING * TAP_ROWS, outer), BF16),
            pltpu.VMEM((channels, outer), BF16),
            pltpu.SemaphoreType.DMA((planes,)),
        ],
        2 * flops,
        4 * channels * outer,
        "conv_backward",
        (),
        (0,),
    )
    backs = [to_slot(value, slot) for slot, value in enumerate(backs)]
    got = lax.all_to_all(part.reshape(parts, block, outer), "filt", 0, 0, tiled=True)
    filt, activation = call(
        functools.partial(unpack_kernel, planes),
        (*backs,),
        [((TAP_ROWS, WIDE), BF16), ((block, voxels), BF16)],
        [],
        UNPACK,
        RING * TAP_ROWS * WIDE * 2,
        "unpack",
    )
    by = lambda m: [(i, i ^ m) for i in range(slabs)]
    other = lax.ppermute(filt, "space", by(1))
    filt = (filt.astype(F32) + other.astype(F32)).astype(BF16)
    other = lax.ppermute(filt, "space", by(2))
    input_grad, weight_grad = call(
        functools.partial(collect_kernel, planes, 1.0 / math.sqrt(planes * slabs * PLANE)),
        (got, filt, other),
        [((block, voxels), BF16), ((len(TAPS) * block, channels), F32)],
        [],
        0,
        2 * channels * outer,
        "collect",
    )
    weight_grad = weight_grad.reshape(len(TAPS), block, channels)
    shape = features.shape
    return (
        activation.reshape(shape),
        input_grad.reshape(shape),
        jnp.transpose(weight_grad, (1, 0, 2)),
    )


def solution(mesh):
    return jax.shard_map(
        per_device,
        mesh=mesh,
        in_specs=(
            P("filt", "space", None),
            P("filt", None, None),
            P("filt"),
            P("filt", "space", None),
        ),
        out_specs=(P("filt", "space", None), P("filt", "space", None), P("filt", None, None)),
        check_vma=False,
    )
```

```python
import functools
import math

import jax
import jax.numpy as jnp
from jax import lax
from jax.experimental import pallas as pl
from jax.experimental.pallas import tpu as pltpu
from jax.sharding import PartitionSpec as P

H = 32
W = 64
PLANE = H * W
TAPS = [(kd, kh, kw) for kd in (-1, 0, 1) for kh in (-1, 0, 1) for kw in (-1, 0, 1)]
RING = 4
ROWS = H // RING
INNER = ROWS * W
OUTER = INNER + 2 * W
BLOCK = 8
GROUP = RING * BLOCK
WIDE = 256
TAP_ROWS = 224
PACK = 0
PREPARE = 8 * 10**9
UNPACK = 16 * 10**9
F32 = jnp.float32
BF16 = jnp.bfloat16


def moved(x, shift):
    return pltpu.roll(x, shift % x.shape[-1], x.ndim - 1) if shift else x


def fold(x):
    return jnp.concatenate([x[:, :WIDE], x[:, WIDE:]], axis=0)


def unfold(x):
    return jnp.concatenate([x[:BLOCK], x[BLOCK:]], axis=1)


def inside_row(rows, kw):
    col = lax.broadcasted_iota(jnp.int32, (rows, OUTER), 1) % W
    return (col + kw >= 0) & (col + kw < W)


def hop(slot, core):
    return (0, 1 + 2 * core, 2, 3 - 2 * core)[slot]


def ring_chunk(slot):
    at = jnp.bitwise_and(lax.axis_index("filt"), RING - 1)
    core = jnp.bitwise_and(lax.axis_index("space"), 1)
    return jnp.bitwise_xor(at, hop(slot, core))


def swapped(x):
    return jnp.concatenate([x[slot * BLOCK : (slot + 1) * BLOCK] for slot in (0, 3, 2, 1)], 0)


def pack_kernel(planes, x_any, cot_any, bias_any, chunks_any, *refs):
    packs, (x_ref, cot_ref, bias_ref, chunks, in_sems, out_sems) = refs[:RING], refs[RING:]
    sent = []
    copies = [
        pltpu.make_async_copy(src, dst, in_sems.at[i])
        for i, (src, dst) in enumerate(((x_any, x_ref), (cot_any, cot_ref), (bias_any, bias_ref)))
    ]
    for copy in copies:
        copy.start()
    copies[0].wait()
    lane = lax.broadcasted_iota(jnp.int32, (BLOCK, 2 * W), 1)
    for v in range(RING):
        for d in range(planes):
            base = d * PLANE + v * INNER
            halo = jnp.zeros((BLOCK, 2 * W), F32)
            if v < RING - 1:
                below = x_ref[:, base + INNER : base + INNER + 2 * W].astype(F32)
                halo = jnp.where(lane < W, below, halo)
            if v > 0:
                above = x_ref[:, base - 2 * W : base].astype(F32)
                halo = jnp.where(lane < W, halo, above)
            own, halo = x_ref[:, base : base + INNER], halo.astype(BF16)
            for g in range(chunks.shape[1]):
                chunks[v, g, :, d * OUTER : d * OUTER + INNER] = own
                chunks[v, g, :, d * OUTER + INNER : (d + 1) * OUTER] = halo
        sent.append(pltpu.make_async_copy(chunks.at[v], chunks_any.at[:, v], out_sems.at[v]))
        sent[-1].start()
    copies[1].wait()
    copies[2].wait()
    bias = jnp.broadcast_to(bias_ref[...].astype(F32), (16, BLOCK))
    bias = jnp.concatenate([bias, jnp.zeros((16, WIDE - BLOCK), F32)], 1).astype(BF16)
    for slot, pack in enumerate(packs):
        for d in range(planes):
            start = ring_chunk(slot) * INNER + d * PLANE
            rows = cot_ref[:, pl.ds(pl.multiple_of(start, INNER), INNER)]
            pack[16 * d : 16 * d + 16, :] = fold(rows.astype(F32)).astype(BF16)
        pack[16 * planes : 16 * planes + 16, :] = bias
    for copy in sent:
        copy.wait()


def odd_slab():
    return jnp.bitwise_and(lax.axis_index("space"), 1) == 1


def upstream(packs, d):
    rows = slice(16 * d, 16 * d + 16)
    return jnp.concatenate([unfold(pack[rows, :].astype(F32)) for pack in packs], 0)


def offsets(packs, planes):
    diagonal = lax.broadcasted_iota(jnp.int32, (BLOCK, 2 * W), 0) == lax.broadcasted_iota(
        jnp.int32, (BLOCK, 2 * W), 1
    )
    rows = slice(16 * planes, 16 * planes + 16)
    columns = []
    for pack in packs:
        row = pack[rows, 0 : 2 * W].astype(F32)[:BLOCK]
        columns.append(jnp.sum(jnp.where(diagonal, row, 0.0), axis=1, keepdims=True))
    return jnp.concatenate(columns, 0)


def prepare_kernel(*refs):
    taps, (w_ref, turned_ref) = refs[:RING], refs[RING:]
    w = [ref[...].astype(F32) for ref in taps]
    for t in range(len(TAPS)):
        rows = [x[t * BLOCK : (t + 1) * BLOCK] for x in w]
        w_ref[t * GROUP : (t + 1) * GROUP, :] = jnp.concatenate(rows, 0).astype(BF16)
    end = len(TAPS) * GROUP
    w_ref[end:, :] = jnp.zeros((w_ref.shape[0] - end, WIDE), BF16)
    turned_ref[...] = w_ref[...].T


def forward_kernel(planes, x_ref, w_ref, *refs):
    packs, (own_ref, low_ref, high_ref, far_ref, near_ref) = refs[:RING], refs[RING : RING + 5]
    maps, down_ref, up_ref = refs[RING + 5 :]
    maps[...] = jnp.dot(w_ref[...], x_ref[...], preferred_element_type=F32)
    masks = {kw: inside_row(GROUP, kw) for kw in (-1, 1)}
    for out in range(-1, planes + 1):
        total = None
        for kh in (-1, 0, 1):
            line = None
            for kw in (-1, 0, 1):
                term = None
                for kd in (-1, 0, 1):
                    d = out + kd
                    if 0 <= d < planes:
                        at = TAPS.index((kd, kh, kw)) * GROUP
                        part = maps[at : at + GROUP, d * OUTER : (d + 1) * OUTER]
                        term = part if term is None else term + part
                if kw:
                    term = jnp.where(masks[kw], moved(term, -kw), 0.0)
                line = term if line is None else line + term
            line = moved(line, -kh * W)
            total = line if total is None else total + line
        total = total[:, :INNER]
        if out < 0:
            low_ref[...] = total
            down_ref[:, 0:INNER] = total
        elif out >= planes:
            high_ref[...] = total
            up_ref[:, 0:INNER] = total
        else:
            own_ref[:, out * INNER : (out + 1) * INNER] = total
        for edge, ref in ((planes - 1, up_ref), (0, down_ref)):
            if out == edge:
                ref[:, INNER : 2 * INNER] = total
                ref[:, 2 * INNER : 3 * INNER] = upstream(packs, out)
    down, up = down_ref[...], up_ref[...]
    near_ref[...] = jnp.where(odd_slab(), down, up).astype(BF16)
    far_ref[...] = jnp.where(odd_slab(), up, down).astype(BF16)


def backward_kernel(
    planes, x_ref, own_ref, low_ref, high_ref, far_ref, near_ref, turned_ref, *refs
):
    packs, part_any, backs = refs[:RING], refs[RING], refs[RING + 1 : 2 * RING + 1]
    shifted, part, sems = refs[2 * RING + 1 :]
    bias = offsets(packs, planes)
    near, far = swapped(near_ref[...].astype(F32)), swapped(far_ref[...].astype(F32))
    before, after = jnp.where(odd_slab(), near, far), jnp.where(odd_slab(), far, near)
    masks = {kw: inside_row(GROUP, kw) for kw in (-1, 1)}
    end = len(TAPS) * GROUP
    shifted[end:, :] = jnp.zeros((shifted.shape[0] - end, planes * OUTER), BF16)
    for src in range(-1, planes + 1):
        if src < 0:
            pre = before[:, INNER : 2 * INNER] + low_ref[...]
            cot = before[:, 2 * INNER : 3 * INNER]
        elif src >= planes:
            pre = after[:, INNER : 2 * INNER] + high_ref[...]
            cot = after[:, 2 * INNER : 3 * INNER]
        else:
            pre = own_ref[:, src * INNER : (src + 1) * INNER]
            cot = upstream(packs, src)
            if src == 0:
                pre = pre + before[:, 0:INNER]
            if src == planes - 1:
                pre = pre + after[:, 0:INNER]
        pre = pre + bias
        s = jax.nn.sigmoid(pre)
        if 0 <= src < planes:
            act = pre * s
            at = TAP_ROWS + 16 * src
            for m in range(RING):
                rows = act[m * BLOCK : (m + 1) * BLOCK]
                backs[m][at : at + 16, :] = fold(rows).astype(BF16)
        grad = (cot * (s * (1.0 + pre * (1.0 - s)))).astype(BF16).astype(F32)
        grad = jnp.concatenate([grad, jnp.zeros((grad.shape[0], 2 * W), F32)], 1)
        for kh in (-1, 0, 1):
            line = moved(grad, kh * W)
            for kw in (-1, 0, 1):
                term = line
                if kw:
                    term = jnp.where(masks[-kw], moved(line, kw), 0.0)
                term = term.astype(BF16)
                for kd in (-1, 0, 1):
                    d = src + kd
                    if 0 <= d < planes:
                        at = TAPS.index((kd, kh, kw)) * GROUP
                        shifted[at : at + GROUP, d * OUTER : (d + 1) * OUTER] = term
    copies = []
    for d in range(planes):
        lanes = slice(d * OUTER, (d + 1) * OUTER)
        total = jnp.dot(turned_ref[...], shifted[:, lanes], preferred_element_type=F32)
        part[:, lanes] = total.astype(BF16)
        copies.append(pltpu.make_async_copy(part.at[:, lanes], part_any.at[:, lanes], sems.at[d]))
        copies[-1].start()
    filt = lax.dot_general(
        shifted[...], x_ref[...], (((1,), (1,)), ((), ())), preferred_element_type=F32
    )
    for m in range(RING):
        rows = [t * GROUP + m * BLOCK for t in range(len(TAPS))]
        pieces = [filt[at : at + BLOCK] for at in rows] + [jnp.zeros((BLOCK, WIDE), F32)]
        backs[m][0:TAP_ROWS, :] = jnp.concatenate(pieces, 0).astype(BF16)
    for copy in copies:
        copy.wait()


def unpack_kernel(planes, *refs):
    backs, (filt_ref, act_ref) = refs[:RING], refs[RING:]
    total = None
    for m, back in enumerate(backs):
        part = back[0:TAP_ROWS, :].astype(F32)
        total = part if total is None else total + part
        chunk = ring_chunk(m)
        for d in range(planes):
            lanes = pl.ds(pl.multiple_of(chunk * INNER + d * PLANE, INNER), INNER)
            start = TAP_ROWS + 16 * d
            act_ref[:, lanes] = unfold(back[start : start + 16, :].astype(F32)).astype(BF16)
    filt_ref[...] = total.astype(BF16)


def collect_kernel(planes, scale, got_ref, filt_ref, other_ref, out_ref, weight_ref):
    rows = weight_ref.shape[0]
    filt = filt_ref[...].astype(F32) + other_ref[...].astype(F32)
    weight_ref[...] = (filt * scale)[:rows]
    lane = lax.broadcasted_iota(jnp.int32, (BLOCK, 2 * W), 1)
    for d in range(planes):
        sums = []
        for v in range(RING):
            total = None
            for g in range(got_ref.shape[0] // RING):
                part = got_ref[g * RING + v, :, d * OUTER : (d + 1) * OUTER].astype(F32)
                total = part if total is None else total + part
            sums.append(total)
        for v in range(RING):
            first, last = sums[v][:, : 2 * W], sums[v][:, INNER - 2 * W : INNER]
            if v > 0:
                first = first + jnp.where(lane < W, sums[v - 1][:, INNER:], 0.0)
            if v < RING - 1:
                last = last + jnp.where(lane < W, 0.0, sums[v + 1][:, INNER:])
            whole = jnp.concatenate([first, sums[v][:, 2 * W : INNER - 2 * W], last], 1)
            base = d * PLANE + v * INNER
            out_ref[:, base : base + INNER] = whole.astype(BF16)


def call(kernel, ins, outs, scratch, flops, moved_bytes, name, hbm=(), outs_hbm=(), limit=48):
    smem = pl.BlockSpec(memory_space=pltpu.SMEM)
    vmem = pl.BlockSpec(memory_space=pltpu.VMEM)
    anywhere = pl.BlockSpec(memory_space=pl.ANY)
    shapes = tuple(jax.ShapeDtypeStruct(shape, kind) for shape, kind in outs)
    return pl.pallas_call(
        kernel,
        out_shape=shapes,
        in_specs=[smem if x.dtype == jnp.int32 else anywhere if i in hbm else vmem for i, x in enumerate(ins)],
        out_specs=tuple(anywhere if i in outs_hbm else vmem for i in range(len(outs))),
        scratch_shapes=scratch,
        compiler_params=pltpu.CompilerParams(vmem_limit_bytes=limit * 2**20),
        cost_estimate=pl.CostEstimate(flops=flops, bytes_accessed=moved_bytes, transcendentals=0),
        name=name,
    )(*ins)


def per_device(features, weight, bias_vec, cotangent):
    block, planes, _ = features.shape
    channels = weight.shape[2]
    parts = lax.axis_size("filt")
    slabs = lax.axis_size("space")
    voxels = planes * PLANE
    outer = planes * OUTER
    inner = planes * INNER
    group = RING * BLOCK
    w = jnp.transpose(weight, (1, 0, 2)).reshape(len(TAPS) * block, channels)

    def to_slot(value, slot):
        pairs = [
            (s * parts + f, s * parts + (f ^ hop(slot, s & 1)))
            for s in range(slabs)
            for f in range(parts)
        ]
        return lax.ppermute(value, ("space", "filt"), pairs) if slot else value

    first, second = to_slot(w, 1), to_slot(w, 2)
    pack = ((16 * planes + 16, WIDE), BF16)
    chunks, *packs = call(
        functools.partial(pack_kernel, planes),
        (features.reshape(block, voxels), cotangent.reshape(block, voxels), bias_vec[None]),
        [((parts // RING, RING, block, outer), BF16)] + [pack] * RING,
        [
            pltpu.VMEM((block, voxels), BF16),
            pltpu.VMEM((block, voxels), BF16),
            pltpu.VMEM((1, block), BF16),
            pltpu.VMEM((RING, parts // RING, block, outer), BF16),
            pltpu.SemaphoreType.DMA((3,)),
            pltpu.SemaphoreType.DMA((RING,)),
        ],
        PACK,
        2 * parts * block * outer,
        "pack",
        (0, 1, 2),
        (0,),
        61,
    )
    chunks = chunks.reshape(parts, block, outer)
    packs = [to_slot(value, slot) for slot, value in enumerate(packs)]
    third = lax.ppermute(first, "space", [(s, s ^ 1) for s in range(slabs)])
    x = lax.all_to_all(chunks, "filt", 0, 0, tiled=True).reshape(channels, outer)

    edge = ((group, 3 * INNER), BF16)
    plane = ((group, INNER), F32)
    flops = 2 * RING * TAP_ROWS * channels * outer
    w, turned = call(
        prepare_kernel,
        (w, first, second, third),
        [((RING * TAP_ROWS, channels), BF16), ((channels, RING * TAP_ROWS), BF16)],
        [],
        PREPARE,
        RING * TAP_ROWS * WIDE * 4,
        "prepare",
    )
    own, low, high, far, near = call(
        functools.partial(forward_kernel, planes),
        (x, w, *packs),
        [((group, inner), F32), plane, plane, edge, edge],
        [pltpu.VMEM((RING * TAP_ROWS, outer), F32)] + [pltpu.VMEM((group, 3 * INNER), F32)] * 2,
        flops,
        2 * channels * outer,
        "conv_forward",
    )
    inner_slabs = [(s, s + 1 - 2 * (1 - s % 2)) for s in range(1, slabs - 1)]
    far = lax.ppermute(far, "space", inner_slabs)
    near = lax.ppermute(near, "space", [(s, s ^ 1) for s in range(slabs)])
    back = ((TAP_ROWS + 16 * planes, WIDE), BF16)
    part, *backs = call(
        functools.partial(backward_kernel, planes),
        (x, own, low, high, far, near, turned, *packs),
        [((channels, outer), BF16)] + [back] * RING,
        [
            pltpu.VMEM((RING * TAP_ROWS, outer), BF16),
            pltpu.VMEM((channels, outer), BF16),
            pltpu.SemaphoreType.DMA((planes,)),
        ],
        2 * flops,
        4 * channels * outer,
        "conv_backward",
        (),
        (0,),
    )
    backs = [to_slot(value, slot) for slot, value in enumerate(backs)]
    got = lax.all_to_all(part.reshape(parts, block, outer), "filt", 0, 0, tiled=True)
    filt, activation = call(
        functools.partial(unpack_kernel, planes),
        (*backs,),
        [((TAP_ROWS, WIDE), BF16), ((block, voxels), BF16)],
        [],
        UNPACK,
        RING * TAP_ROWS * WIDE * 2,
        "unpack",
    )
    by = lambda m: [(i, i ^ m) for i in range(slabs)]
    other = lax.ppermute(filt, "space", by(1))
    filt = (filt.astype(F32) + other.astype(F32)).astype(BF16)
    other = lax.ppermute(filt, "space", by(2))
    input_grad, weight_grad = call(
        functools.partial(collect_kernel, planes, 1.0 / math.sqrt(planes * slabs * PLANE)),
        (got, filt, other),
        [((block, voxels), BF16), ((len(TAPS) * block, channels), F32)],
        [],
        0,
        2 * channels * outer,
        "collect",
    )
    weight_grad = weight_grad.reshape(len(TAPS), block, channels)
    shape = features.shape
    return (
        activation.reshape(shape),
        input_grad.reshape(shape),
        jnp.transpose(weight_grad, (1, 0, 2)),
    )


def solution(mesh):
    return jax.shard_map(
        per_device,
        mesh=mesh,
        in_specs=(
            P("filt", "space", None),
            P("filt", None, None),
            P("filt"),
            P("filt", "space", None),
        ),
        out_specs=(P("filt", "space", None), P("filt", "space", None), P("filt", None, None)),
        check_vma=False,
    )
```
